32 devices in a mesh: section: 2 (over x), fsdp: 4 (over y, core), tp: 4 (over z).
Axes of the slice: x: 2, y: 2, z: 4, core: 2. Of those that a mesh axis runs over, the one named last changes fastest.
Arguments:
- queries: bfloat16 [2, 512, 4096], P('section', 'fsdp', 'tp'), may hold values from -160 to 160
- key_rows: bfloat16 [2, 512, 512], P('section', 'fsdp', 'tp'), may hold values from -8 to 8
- values: bfloat16 [2, 512, 512], P('section', 'fsdp', 'tp'), may hold values from -6 to 6
- segments: int32 [2, 512], P('section', 'fsdp'), may hold values from 0 to 3, never falling along the last dimension, each value on 1 to 384 neighbouring positions
- held_queries: bfloat16 [2, 512, 4096], P('section', ('fsdp', 'tp')), may hold values from -160 to 160
- held_keys: bfloat16 [2, 512, 512], P('section', ('fsdp', 'tp')), may hold values from -8 to 8
- held_values: bfloat16 [2, 512, 512], P('section', ('fsdp', 'tp')), may hold values from -6 to 6
- held_segments: int32 [2, 512], P('section', 'fsdp'), may hold values from 0 to 3, never falling along the last dimension, each value on 1 to 384 neighbouring positions
- out_grad: bfloat16 [2, 512, 4096], P('section', 'fsdp', 'tp'), may hold values from -6 to 6
Outputs:
- attn_out: bfloat16 [2, 512, 4096], P('section', 'fsdp', 'tp')
- query_grad: bfloat16 [2, 512, 4096], P('section', 'fsdp', 'tp')
- key_grad: bfloat16 [2, 512, 512], P('section', 'fsdp', 'tp')
- value_grad: bfloat16 [2, 512, 512], P('section', 'fsdp', 'tp')
The draws below stay inside these ranges and needn't reach their ends.
All inputs are finite; a program needn't handle non-finite values.
Results may differ from the reference program's by a relative error of at most 0.014.
Values may be sent and summed in bfloat16 or wider, within the bound.
A program may use at most 64 MiB of HBM per device.

```python
import math
import jax
import jax.numpy as jnp
import numpy as np
from jax import lax

TOK_DEV = 128
HEADS = 32
KV_HEADS = 4
HEAD_DIM = 128
SECTIONS = 2
SEQ = 512
N_FSDP = 4


def paired_draw(key, salt):
    base_key = jax.random.fold_in(key, salt)
    key_field = jax.random.normal(jax.random.fold_in(base_key, 1), (SECTIONS, SEQ, KV_HEADS, HEAD_DIM), jnp.float32)
    query_field = jax.random.normal(jax.random.fold_in(base_key, 2), (SECTIONS, SEQ, KV_HEADS, HEADS // KV_HEADS, HEAD_DIM), jnp.float32)
    return (query_field, key_field)


def draw_queries(key, part):
    query_field, key_field = paired_draw(key, 5)
    return query_field.reshape(SECTIONS, SEQ, HEADS * HEAD_DIM).astype(jnp.bfloat16)


def draw_key_rows(key, part):
    query_field, key_field = paired_draw(key, 5)
    return key_field.reshape(SECTIONS, SEQ, KV_HEADS * HEAD_DIM).astype(jnp.bfloat16)


def draw_held_queries(key, part):
    query_field, key_field = paired_draw(key, 7)
    return query_field.reshape(SECTIONS, SEQ, HEADS * HEAD_DIM).astype(jnp.bfloat16)


def draw_held_keys(key, part):
    query_field, key_field = paired_draw(key, 7)
    return key_field.reshape(SECTIONS, SEQ, KV_HEADS * HEAD_DIM).astype(jnp.bfloat16)


def block_scale(stream_key, dims, cuts, smallest, high):
    factor_of, own = 1.0, jax.random.fold_in(stream_key, 6)
    for dim, shards_of in cuts:
        draws = jnp.exp(jax.random.uniform(jax.random.fold_in(own, dim), (shards_of,), jnp.float32, smallest / len(cuts), high / len(cuts)))
        factor_of = factor_of * jnp.repeat(draws, dims[dim] // shards_of).reshape([-1 if axis == dim else 1 for axis in range(len(dims))])
    return factor_of


def split_up(number_of, total, most, skew):
    portions = [(1 << 20) // math.isqrt(standing ** skew) + 1 for standing in range(2, number_of + 1)]
    surplus, given = total - most - (number_of - 1), [1] * (number_of - 1)
    while surplus > 0:
        movable = [i for i in range(number_of - 1) if given[i] < most]
        whole, left = sum([portions[i] for i in movable]), surplus
        for i in movable:
            extra = min(most - given[i], max(1, left * portions[i] // whole), surplus)
            given[i] = given[i] + extra
            surplus = surplus - extra
    return np.array([most] + given)


def ragged_sizes(stream_key, amount, total, most, slope):
    if amount == 2:
        one = jax.random.randint(stream_key, (), max(1, total - most), min(most, total - 1) + 1)
        return jnp.stack([one, total - one])
    lengths = jnp.asarray(split_up(amount, total, most, slope), jnp.int32)
    twos = (amount - 1) // 2
    source_of, receiver = lengths[1:1 + 2 * twos:2], lengths[2:2 + 2 * twos:2]
    margin = jnp.minimum(source_of - 1, most - receiver)
    moved = jax.random.randint(jax.random.fold_in(stream_key, 1), (twos,), 0, 1 << 20) % (margin + 1)
    lengths = lengths.at[1:1 + 2 * twos:2].set(source_of - moved).at[2:2 + 2 * twos:2].set(receiver + moved)
    return lengths[jax.random.permutation(jax.random.fold_in(stream_key, 2), amount)]


def centred(own_key, shape, width, reach, cuts=(), held_as=jnp.bfloat16):
    level = block_scale(own_key, shape, cuts, -0.22, 0.18) if cuts else 1.0
    entries = jax.random.normal(own_key, shape, jnp.float32) * width * level
    return jnp.minimum(jnp.maximum(entries, -reach), reach).astype(held_as)


def setup_inputs(seed: int = 0) -> dict:
    key_of = jax.random.split(jax.random.key(seed), 10)
    queries = draw_queries(jax.random.fold_in(key_of[9], 71), 0)
    key_rows = draw_key_rows(jax.random.fold_in(key_of[9], 71), 0)
    values = centred(key_of[2], (SECTIONS, SEQ, KV_HEADS * HEAD_DIM), 1.0, 6.0, ((0, 2), (1, 4), (2, 4)))
    segments = jax.vmap(lambda own: jnp.searchsorted(jnp.cumsum(ragged_sizes(own, N_FSDP, SEQ, SEQ // 2 + TOK_DEV, 2)), jnp.arange(SEQ), side="right"))(jax.random.split(key_of[3], SECTIONS)).reshape((SECTIONS, SEQ)).astype(jnp.int32)
    held_queries = draw_held_queries(jax.random.fold_in(key_of[9], 71), 0)
    held_keys = draw_held_keys(jax.random.fold_in(key_of[9], 71), 0)
    held_values = centred(key_of[6], (SECTIONS, SEQ, KV_HEADS * HEAD_DIM), 1.0, 6.0, ((0, 2), (1, 16)))
    held_segments = jax.vmap(lambda own: jnp.searchsorted(jnp.cumsum(ragged_sizes(own, N_FSDP, SEQ, SEQ // 2 + TOK_DEV, 2)), jnp.arange(SEQ), side="right"))(jax.random.split(key_of[7], SECTIONS)).reshape((SECTIONS, SEQ)).astype(jnp.int32)
    out_grad = centred(key_of[8], (SECTIONS, SEQ, HEADS * HEAD_DIM), 1.0, 6.0, ((0, 2), (1, 4), (2, 4)))
    return dict(queries=queries, key_rows=key_rows, values=values, segments=segments, held_queries=held_queries, held_keys=held_keys, held_values=held_values, held_segments=held_segments, out_grad=out_grad)


NEG = -1e+30

def visible_pairs(seg_row):
    position = jnp.arange(seg_row.shape[0], dtype=jnp.int32)
    return (position[None, :] <= position[:, None]) & (seg_row[None, :] == seg_row[:, None])

def lowered(array):
    return lax.optimization_barrier(array.astype(jnp.bfloat16)).astype(jnp.float32)

def group_scores(query_group, key_group):
    scores = jnp.einsum('ird,jd->irj', query_group.astype(jnp.float32), key_group.astype(jnp.float32), precision=lax.Precision.HIGHEST)
    return scores * (1.0 / math.sqrt(HEAD_DIM))

def group_forward(query_group, key_group, value_group, visible):
    visible_wide = visible[:, None, :]
    scores = jnp.where(visible_wide, group_scores(query_group, key_group), NEG)
    row_max = lax.optimization_barrier(jnp.max(scores, axis=-1))
    weights = jnp.where(visible_wide, jnp.exp(scores - row_max[..., None]), 0.0)
    row_sum = lax.optimization_barrier(jnp.sum(weights, axis=-1))
    numerator = jnp.einsum('irj,jd->ird', lowered(weights), value_group.astype(jnp.float32), precision=lax.Precision.HIGHEST)
    return (numerator / row_sum[..., None], row_max + jnp.log(row_sum))

def group_backward(query_group, key_group, value_group, grad_group, visible):
    outputs, log_total = group_forward(query_group, key_group, value_group, visible)
    grad_wide = grad_group.astype(jnp.float32)
    delta_rows = lax.optimization_barrier(jnp.sum(grad_wide * outputs, axis=-1))
    visible_wide = visible[:, None, :]
    scores = group_scores(query_group, key_group)
    probabilities = jnp.where(visible_wide, jnp.exp(scores - log_total[..., None]), 0.0)
    value_part = jnp.einsum('irj,ird->jd', lowered(probabilities), grad_wide, precision=lax.Precision.HIGHEST)
    prob_grad = jnp.einsum('ird,jd->irj', grad_wide, value_group.astype(jnp.float32), precision=lax.Precision.HIGHEST)
    score_grad = lowered(probabilities * (prob_grad - delta_rows[..., None]))
    score_scale = 1.0 / math.sqrt(HEAD_DIM)
    query_part = jnp.einsum('irj,jd->ird', score_grad, key_group.astype(jnp.float32), precision=lax.Precision.HIGHEST) * score_scale
    key_part = jnp.einsum('irj,ird->jd', score_grad, query_group.astype(jnp.float32), precision=lax.Precision.HIGHEST) * score_scale
    return (query_part.astype(jnp.bfloat16), key_part.astype(jnp.bfloat16), value_part.astype(jnp.bfloat16))

def split_heads(query_section, key_section, value_section):
    group_ratio = HEADS // KV_HEADS
    query_split = query_section.reshape(SEQ, KV_HEADS, group_ratio, HEAD_DIM).transpose(1, 0, 2, 3)
    key_split = key_section.reshape(SEQ, KV_HEADS, HEAD_DIM).transpose(1, 0, 2)
    value_split = value_section.reshape(SEQ, KV_HEADS, HEAD_DIM).transpose(1, 0, 2)
    return (query_split, key_split, value_split)

def section_forward(section_items):
    query_section, key_section, value_section, seg_section = section_items
    visible = visible_pairs(seg_section)
    query_split, key_split, value_split = split_heads(query_section, key_section, value_section)

    def one_group(group_items):
        return group_forward(group_items[0], group_items[1], group_items[2], visible)[0]
    outputs = lax.map(one_group, (query_split, key_split, value_split))
    return outputs.transpose(1, 0, 2, 3).reshape(SEQ, HEADS * HEAD_DIM).astype(jnp.bfloat16)

def section_backward(section_items):
    query_section, key_section, value_section, seg_section, grad_section = section_items
    visible = visible_pairs(seg_section)
    query_split, key_split, value_split = split_heads(query_section, key_section, value_section)
    grad_split = grad_section.reshape(SEQ, KV_HEADS, HEADS // KV_HEADS, HEAD_DIM).transpose(1, 0, 2, 3)

    def one_group(group_items):
        return group_backward(group_items[0], group_items[1], group_items[2], group_items[3], visible)
    query_part, key_part, value_part = lax.map(one_group, (query_split, key_split, value_split, grad_split))
    query_grad = query_part.transpose(1, 0, 2, 3).reshape(SEQ, HEADS * HEAD_DIM)
    key_grad = key_part.transpose(1, 0, 2).reshape(SEQ, KV_HEADS * HEAD_DIM)
    value_grad = value_part.transpose(1, 0, 2).reshape(SEQ, KV_HEADS * HEAD_DIM)
    return (query_grad, key_grad, value_grad)

def reference(queries, key_rows, values, segments, held_queries, held_keys, held_values, held_segments, out_grad):
    attn_out = lax.map(section_forward, (queries, key_rows, values, segments))
    reloaded = (held_queries[::-1], held_keys[::-1], held_values[::-1], held_segments[::-1], out_grad)
    query_grad, key_grad, value_grad = lax.map(section_backward, reloaded)
    return (attn_out, query_grad, key_grad, value_grad)
```

```python
import functools
import math

import jax
import jax.numpy as jnp
from jax import lax
from jax.experimental import pallas as pl
from jax.experimental.pallas import tpu as pltpu
from jax.sharding import PartitionSpec as P

HEAD_DIM = 128
PAIR = 2
NEG = -1e30
SCALE = 1.0 / math.sqrt(HEAD_DIM)
SCALE_LOG2 = SCALE * math.log2(math.e)
MESH = pl.DeviceIdType.MESH

NT = (((1,), (1,)), ((), ()))


def dot(left, right, dims=(((1,), (0,)), ((), ()))):
    return lax.dot_general(left, right, dims, preferred_element_type=jnp.float32)


def kernel(
    n_s,
    n_f,
    n_t,
    q_ref,
    k_ref,
    v_ref,
    sg_ref,
    hq_ref,
    hk_ref,
    hv_ref,
    hs_ref,
    do_ref,
    o_ref,
    dq_ref,
    dk_ref,
    dv_ref,
    q_buf,
    g_buf,
    kv_fwd,
    sg_fwd,
    hq_buf,
    kv_held,
    sg_held,
    bias,
    turned,
    s_buf,
    p_buf,
    dk_acc,
    dv_acc,
    part_out,
    part_in,
    o_buf,
    dq_buf,
    dk_buf,
    dv_buf,
    local_sem,
    fwd_send,
    fwd_recv,
    one_send,
    one_recv,
    two_send,
    two_recv,
    hq_send,
    hq_recv,
    red_send,
    red_recv,
):
    rows = q_ref.shape[1]
    part_rows = hq_ref.shape[1]
    width = q_ref.shape[2]
    pair_width = PAIR * HEAD_DIM
    pairs = width // pair_width
    seq = n_f * rows
    block = min(512, seq)
    blocks = seq // block

    s, f, t = lax.axis_index("section"), lax.axis_index("fsdp"), lax.axis_index("tp")
    mirror = n_s - 1 - s

    def at_f(step):
        return lax.rem(f + step, n_f)

    def at_t(step):
        return lax.rem(t + step, n_t)

    local = [
        pltpu.make_async_copy(k_ref.at[0], kv_fwd.at[f, 0], local_sem.at[0]),
        pltpu.make_async_copy(v_ref.at[0], kv_fwd.at[f, 1], local_sem.at[1]),
        pltpu.make_async_copy(sg_ref, sg_fwd.at[f], local_sem.at[2]),
        pltpu.make_async_copy(q_ref.at[0], q_buf, local_sem.at[3]),
        pltpu.make_async_copy(do_ref.at[0], g_buf, local_sem.at[4]),
    ]
    for copy in local:
        copy.start()

    barrier = pltpu.get_barrier_semaphore()
    for step in range(n_t):
        pl.semaphore_signal(
            barrier, inc=1, device_id=(mirror, f, at_t(step)), device_id_type=MESH
        )
    for step in range(1, n_f):
        pl.semaphore_signal(barrier, inc=1, device_id=(s, at_f(step), t), device_id_type=MESH)
    pl.semaphore_wait(barrier, n_t + n_f - 1)

    def remote(src, dst, send_sem, recv_sem, device):
        return pltpu.make_async_remote_copy(
            src_ref=src,
            dst_ref=dst,
            send_sem=send_sem,
            recv_sem=recv_sem,
            device_id=device,
            device_id_type=MESH,
        )

    own_rows = pl.ds(pl.multiple_of(t * part_rows, part_rows), part_rows)

    first = []
    for step in range(n_t):
        to = at_t(step)
        columns = pl.ds(pl.multiple_of(to * HEAD_DIM, HEAD_DIM), HEAD_DIM)
        for which, held in enumerate((hk_ref, hv_ref)):
            first.append(
                remote(
                    held.at[0, :, columns],
                    kv_held.at[f, which, own_rows, :],
                    one_send.at[2 * step + which],
                    one_recv.at[2 * step + which],
                    (mirror, f, to),
                )
            )
    first.append(
        remote(
            hs_ref,
            sg_held.at[f],
            one_send.at[2 * n_t],
            one_recv.at[2 * n_t],
            (mirror, f, t),
        )
    )
    for copy in first:
        copy.start()

    fwd = []
    for step in range(1, n_f):
        device = (s, at_f(step), t)
        at = 3 * (step - 1)
        for which, src in enumerate((k_ref.at[0], v_ref.at[0], sg_ref)):
            dst = sg_fwd.at[f] if which == 2 else kv_fwd.at[f, which]
            fwd.append(
                remote(src, dst, fwd_send.at[at + which], fwd_recv.at[at + which], device)
            )
    for copy in fwd:
        copy.start()

    def query_copy(pair, step):
        to = at_t(step)
        columns = pl.ds(
            pl.multiple_of(to * width + pair * pair_width, pair_width), pair_width
        )
        return remote(
            hq_ref.at[0, :, columns],
            hq_buf.at[pair, own_rows, :],
            hq_send.at[pair, step],
            hq_recv.at[pair, step],
            (mirror, f, to),
        )

    for pair in range(pairs):
        for step in range(n_t):
            query_copy(pair, step).start()

    for copy in first:
        copy.wait_recv()
    second = []
    for step in range(1, n_f):
        device = (s, at_f(step), t)
        at = 2 * (step - 1)
        second.append(
            remote(
                kv_held.at[f], kv_held.at[f], two_send.at[at], two_recv.at[at], device
            )
        )
        second.append(
            remote(
                sg_held.at[f],
                sg_held.at[f],
                two_send.at[at + 1],
                two_recv.at[at + 1],
                device,
            )
        )
    for copy in second:
        copy.start()

    def make_bias(ids):
        own = ids[f]
        for b in range(n_f):
            key_ids = jnp.transpose(jnp.broadcast_to(ids[b], (HEAD_DIM, rows)))[:, :1]
            key_pos = b * rows + lax.broadcasted_iota(jnp.int32, (rows, rows), 0)
            own_pos = f * rows + lax.broadcasted_iota(jnp.int32, (rows, rows), 1)
            seen = (key_pos <= own_pos) & (key_ids == own)
            bias[b * rows : (b + 1) * rows, :] = jnp.where(seen, 0.0, NEG)

    def over_blocks(step, start):
        if blocks == 1:
            return step(0, start)
        return lax.fori_loop(0, blocks, step, start)

    def span(b):
        if blocks == 1:
            return pl.ds(0, block)
        return pl.ds(pl.multiple_of(b * block, block), block)

    def piece(kv, which, b):
        per = block // rows
        if blocks == 1:
            part = kv[:, which]
        else:
            part = kv[pl.ds(b * per, per), which]
        return part.reshape(block, HEAD_DIM)

    def turn(kv, which):
        for b in range(n_f):
            turned[:, b * rows : (b + 1) * rows] = jnp.transpose(kv[b, which])

    def stacked(pair_block):
        return jnp.concatenate(
            [pair_block[:, h * HEAD_DIM : (h + 1) * HEAD_DIM] for h in range(PAIR)], axis=0
        )

    def scores_of(kv, query):
        def step(b, top):
            masked = jnp.concatenate([bias[span(b), :]] * PAIR, axis=1)
            scores = dot(piece(kv, 0, b), query, NT) * SCALE_LOG2 + masked
            s_buf[span(b), :] = scores
            return jnp.maximum(top, jnp.max(scores, axis=0, keepdims=True))

        return over_blocks(step, jnp.full((1, PAIR * rows), NEG, jnp.float32))

    def untangled(wide):
        return jnp.concatenate(
            [
                jnp.transpose(wide[:, h * rows : (h + 1) * rows])
                for h in range(PAIR)
            ],
            axis=1,
        ).astype(jnp.bfloat16)

    def lanes_of(pair):
        return pl.ds(pl.multiple_of(pair * pair_width, pair_width), pair_width)

    for copy in local:
        copy.wait()
    for copy in fwd:
        copy.wait_recv()
    make_bias(sg_fwd)
    turn(kv_fwd, 1)

    def forward_pair(pair, carry):
        query = stacked(q_buf[:, lanes_of(pair)])
        top = scores_of(kv_fwd, query)

        def step(b, sums):
            total, out = sums
            weights = jnp.exp2(s_buf[span(b), :] - top)
            total = total + jnp.sum(weights, axis=0, keepdims=True)
            out = out + dot(turned[:, span(b)], weights.astype(jnp.bfloat16))
            return total, out

        total, out = over_blocks(
            step,
            (
                jnp.zeros((1, PAIR * rows), jnp.float32),
                jnp.zeros((HEAD_DIM, PAIR * rows), jnp.float32),
            ),
        )
        o_buf[:, lanes_of(pair)] = untangled(out * (1.0 / total))
        return carry

    lax.fori_loop(0, pairs, forward_pair, 0)
    out_copy = pltpu.make_async_copy(o_buf, o_ref.at[0], local_sem.at[0])
    out_copy.start()

    for copy in second:
        copy.wait_recv()
    make_bias(sg_held)
    turn(kv_held, 0)
    dk_acc[...] = jnp.zeros_like(dk_acc)
    dv_acc[...] = jnp.zeros_like(dv_acc)

    def backward_pair(pair, carry):
        for step in range(n_t):
            query_copy(pair, step).wait_recv()
        query = stacked(hq_buf[pair])
        grad = stacked(g_buf[:, lanes_of(pair)])
        top = scores_of(kv_held, query)

        def middle(b, sums):
            total, along = sums
            weights = jnp.exp2(s_buf[span(b), :] - top)
            prob_grad = dot(piece(kv_held, 1, b), grad, NT)
            s_buf[span(b), :] = weights
            p_buf[span(b), :] = prob_grad
            total = total + jnp.sum(weights, axis=0, keepdims=True)
            along = along + jnp.sum(weights * prob_grad, axis=0, keepdims=True)
            return total, along

        zero = jnp.zeros((1, PAIR * rows), jnp.float32)
        total, along = over_blocks(middle, (zero, zero))
        inverse = 1.0 / total
        delta = along * inverse

        def last(b, query_sum):
            probs = s_buf[span(b), :] * inverse
            score_grad = (probs * (p_buf[span(b), :] - delta)).astype(jnp.bfloat16)
            dv_acc[span(b), :] += dot(probs.astype(jnp.bfloat16), grad)
            dk_acc[span(b), :] += dot(score_grad, query)
            return query_sum + dot(turned[:, span(b)], score_grad)

        query_sum = over_blocks(last, jnp.zeros((HEAD_DIM, PAIR * rows), jnp.float32))
        dq_buf[:, lanes_of(pair)] = untangled(query_sum * SCALE)
        return carry

    lax.fori_loop(0, pairs, backward_pair, 0)
    query_grad_copy = pltpu.make_async_copy(dq_buf, dq_ref.at[0], local_sem.at[1])
    query_grad_copy.start()

    def rows_at(index):
        return pl.ds(pl.multiple_of(index * rows, rows), rows)

    reduce = []
    for step in range(1, n_f):
        to = at_f(step)
        part_out[step - 1, 0] = dk_acc[rows_at(to), :].astype(jnp.bfloat16)
        part_out[step - 1, 1] = dv_acc[rows_at(to), :].astype(jnp.bfloat16)
        copy = remote(
            part_out.at[step - 1],
            part_in.at[step - 1],
            red_send.at[step - 1],
            red_recv.at[step - 1],
            (s, to, t),
        )
        copy.start()
        reduce.append(copy)
    key_sum = dk_acc[rows_at(f), :]
    value_sum = dv_acc[rows_at(f), :]
    for step in range(1, n_f):
        reduce[step - 1].wait_recv()
        key_sum = key_sum + part_in[step - 1, 0].astype(jnp.float32)
        value_sum = value_sum + part_in[step - 1, 1].astype(jnp.float32)
    dk_buf[...] = (key_sum * SCALE).astype(jnp.bfloat16)
    dv_buf[...] = value_sum.astype(jnp.bfloat16)
    last_copies = [
        pltpu.make_async_copy(dk_buf, dk_ref.at[0], local_sem.at[2]),
        pltpu.make_async_copy(dv_buf, dv_ref.at[0], local_sem.at[3]),
    ]
    for copy in last_copies:
        copy.start()
    for copy in first + fwd + second + reduce:
        copy.wait_send()
    for pair in range(pairs):
        for step in range(n_t):
            query_copy(pair, step).wait_send()
    for copy in [out_copy, query_grad_copy] + last_copies:
        copy.wait()


def local(sizes, *arrays):
    n_s, n_f, n_t = sizes
    queries, key_rows = arrays[0], arrays[1]
    rows, width = queries.shape[1], queries.shape[2]
    pairs = width // (PAIR * HEAD_DIM)
    seq = n_f * rows
    low, full = jnp.bfloat16, jnp.float32
    dma = pltpu.SemaphoreType.DMA
    anywhere = pl.BlockSpec(memory_space=pl.ANY)
    elements = rows * (width // HEAD_DIM) * seq
    return pl.pallas_call(
        functools.partial(kernel, n_s, n_f, n_t),
        out_shape=[
            jax.ShapeDtypeStruct(queries.shape, low),
            jax.ShapeDtypeStruct(queries.shape, low),
            jax.ShapeDtypeStruct(key_rows.shape, low),
            jax.ShapeDtypeStruct(key_rows.shape, low),
        ],
        in_specs=[anywhere] * 9,
        out_specs=[anywhere] * 4,
        scratch_shapes=[
            pltpu.VMEM((rows, width), low),
            pltpu.VMEM((rows, width), low),
            pltpu.VMEM((n_f, 2, rows, HEAD_DIM), low),
            pltpu.VMEM((n_f, 1, rows), jnp.int32),
            pltpu.VMEM((pairs, rows, PAIR * HEAD_DIM), low),
            pltpu.VMEM((n_f, 2, rows, HEAD_DIM), low),
            pltpu.VMEM((n_f, 1, rows), jnp.int32),
            pltpu.VMEM((seq, rows), full),
            pltpu.VMEM((HEAD_DIM, seq), low),
            pltpu.VMEM((seq, PAIR * rows), full),
            pltpu.VMEM((seq, PAIR * rows), full),
            pltpu.VMEM((seq, HEAD_DIM), full),
            pltpu.VMEM((seq, HEAD_DIM), full),
            pltpu.VMEM((n_f - 1, 2, rows, HEAD_DIM), low),
            pltpu.VMEM((n_f - 1, 2, rows, HEAD_DIM), low),
            pltpu.VMEM((rows, width), low),
            pltpu.VMEM((rows, width), low),
            pltpu.VMEM((rows, HEAD_DIM), low),
            pltpu.VMEM((rows, HEAD_DIM), low),
            dma((5,)),
            dma((3 * (n_f - 1),)),
            dma((3 * (n_f - 1),)),
            dma((2 * n_t + 1,)),
            dma((2 * n_t + 1,)),
            dma((2 * (n_f - 1),)),
            dma((2 * (n_f - 1),)),
            dma((pairs, n_t)),
            dma((pairs, n_t)),
            dma((n_f - 1,)),
            dma((n_f - 1,)),
        ],
        compiler_params=pltpu.CompilerParams(
            collective_id=0, has_side_effects=True, vmem_limit_bytes=40 * 1024 * 1024
        ),
        cost_estimate=pl.CostEstimate(
            flops=14 * elements * HEAD_DIM,
            bytes_accessed=6 * rows * width * 2,
            transcendentals=2 * elements,
        ),
        name="tick",
    )(*arrays)


def solution(mesh):
    sizes = (mesh.shape["section"], mesh.shape["fsdp"], mesh.shape["tp"])
    by_head = P("section", "fsdp", "tp")
    by_row = P("section", ("fsdp", "tp"), None)
    ids = P("section", "fsdp")
    return jax.shard_map(
        functools.partial(local, sizes),
        mesh=mesh,
        in_specs=(by_head, by_head, by_head, ids, by_row, by_row, by_row, ids, by_head),
        out_specs=(by_head,) * 4,
        check_vma=False,
    )
```

```python
import functools
import math

import jax
import jax.numpy as jnp
from jax import lax
from jax.experimental import pallas as pl
from jax.experimental.pallas import tpu as pltpu
from jax.sharding import PartitionSpec as P

HEAD_DIM = 128
PAIR = 2
NEG = -1e30
SCALE = 1.0 / math.sqrt(HEAD_DIM)
SCALE_LOG2 = SCALE * math.log2(math.e)
MESH = pl.DeviceIdType.MESH
VMEM_BYTES = 63 * 1024 * 1024

NT = (((1,), (1,)), ((), ()))


def dot(left, right, dims=(((1,), (0,)), ((), ()))):
    return lax.dot_general(left, right, dims, preferred_element_type=jnp.float32)


def kernel(
    n_s,
    n_f,
    n_t,
    q_ref,
    k_ref,
    v_ref,
    sg_ref,
    hq_ref,
    hk_ref,
    hv_ref,
    hs_ref,
    do_ref,
    o_ref,
    dq_ref,
    dk_ref,
    dv_ref,
    q_buf,
    g_buf,
    kv_fwd,
    sg_fwd,
    hq_buf,
    kv_held,
    sg_held,
    bias,
    turned,
    s_buf,
    p_buf,
    p_low,
    d_low,
    q_stack,
    g_stack,
    part_out,
    part_in,
    o_buf,
    dq_buf,
    dk_buf,
    dv_buf,
    local_sem,
    fwd_send,
    fwd_recv,
    one_send,
    one_recv,
    two_send,
    two_recv,
    hq_send,
    hq_recv,
    red_send,
    red_recv,
):
    rows = q_ref.shape[1]
    part_rows = hq_ref.shape[1]
    width = q_ref.shape[2]
    pair_width = PAIR * HEAD_DIM
    pairs = width // pair_width
    seq = n_f * rows
    block = min(512, seq)
    blocks = seq // block

    s, f, t = lax.axis_index("section"), lax.axis_index("fsdp"), lax.axis_index("tp")
    mirror = n_s - 1 - s

    def at_f(step):
        return lax.rem(f + step, n_f)

    def at_t(step):
        return lax.rem(t + step, n_t)

    local = [
        pltpu.make_async_copy(k_ref.at[0], kv_fwd.at[f, 0], local_sem.at[0]),
        pltpu.make_async_copy(v_ref.at[0], kv_fwd.at[f, 1], local_sem.at[1]),
        pltpu.make_async_copy(sg_ref, sg_fwd.at[f], local_sem.at[2]),
        pltpu.make_async_copy(q_ref.at[0], q_buf, local_sem.at[3]),
        pltpu.make_async_copy(do_ref.at[0], g_buf, local_sem.at[4]),
    ]
    for copy in local:
        copy.start()

    barrier = pltpu.get_barrier_semaphore()
    for step in range(n_t):
        pl.semaphore_signal(
            barrier, inc=1, device_id=(mirror, f, at_t(step)), device_id_type=MESH
        )
    for step in range(1, n_f):
        pl.semaphore_signal(barrier, inc=1, device_id=(s, at_f(step), t), device_id_type=MESH)
    pl.semaphore_wait(barrier, n_t + n_f - 1)

    def remote(src, dst, send_sem, recv_sem, device):
        return pltpu.make_async_remote_copy(
            src_ref=src,
            dst_ref=dst,
            send_sem=send_sem,
            recv_sem=recv_sem,
            device_id=device,
            device_id_type=MESH,
        )

    own_rows = pl.ds(pl.multiple_of(t * part_rows, part_rows), part_rows)

    first = []
    for step in range(n_t):
        to = at_t(step)
        columns = pl.ds(pl.multiple_of(to * HEAD_DIM, HEAD_DIM), HEAD_DIM)
        for which, held in enumerate((hk_ref, hv_ref)):
            first.append(
                remote(
                    held.at[0, :, columns],
                    kv_held.at[f, which, own_rows, :],
                    one_send.at[2 * step + which],
                    one_recv.at[2 * step + which],
                    (mirror, f, to),
                )
            )
    first.append(
        remote(
            hs_ref,
            sg_held.at[f],
            one_send.at[2 * n_t],
            one_recv.at[2 * n_t],
            (mirror, f, t),
        )
    )
    for copy in first:
        copy.start()

    fwd = []
    for step in range(1, n_f):
        device = (s, at_f(step), t)
        at = 3 * (step - 1)
        for which, src in enumerate((k_ref.at[0], v_ref.at[0], sg_ref)):
            dst = sg_fwd.at[f] if which == 2 else kv_fwd.at[f, which]
            fwd.append(
                remote(src, dst, fwd_send.at[at + which], fwd_recv.at[at + which], device)
            )
    for copy in fwd:
        copy.start()

    def query_copy(pair, step):
        to = at_t(step)
        columns = pl.ds(
            pl.multiple_of(to * width + pair * pair_width, pair_width), pair_width
        )
        return remote(
            hq_ref.at[0, :, columns],
            hq_buf.at[pair, own_rows, :],
            hq_send.at[pair, step],
            hq_recv.at[pair, step],
            (mirror, f, to),
        )

    for pair in range(pairs):
        for step in range(n_t):
            query_copy(pair, step).start()

    for copy in first:
        copy.wait_recv()
    second = []
    for step in range(1, n_f):
        device = (s, at_f(step), t)
        at = 2 * (step - 1)
        second.append(
            remote(
                kv_held.at[f], kv_held.at[f], two_send.at[at], two_recv.at[at], device
            )
        )
        second.append(
            remote(
                sg_held.at[f],
                sg_held.at[f],
                two_send.at[at + 1],
                two_recv.at[at + 1],
                device,
            )
        )
    for copy in second:
        copy.start()

    def make_bias(ids):
        own = ids[f]
        for b in range(n_f):
            key_ids = jnp.transpose(jnp.broadcast_to(ids[b], (rows, rows)))
            key_pos = b * rows + lax.broadcasted_iota(jnp.int32, (rows, rows), 0)
            own_pos = f * rows + lax.broadcasted_iota(jnp.int32, (rows, rows), 1)
            seen = (key_pos <= own_pos) & (key_ids == own)
            bias[b * rows : (b + 1) * rows, :] = jnp.where(seen, 0.0, NEG)

    def over_blocks(step, start):
        if blocks == 1:
            return step(0, start)
        return lax.fori_loop(0, blocks, step, start)

    def span(b):
        if blocks == 1:
            return pl.ds(0, block)
        return pl.ds(pl.multiple_of(b * block, block), block)

    def piece(kv, which, b):
        per = block // rows
        if blocks == 1:
            part = kv[:, which]
        else:
            part = kv[pl.ds(b * per, per), which]
        return part.reshape(block, HEAD_DIM)

    def turn(kv, which):
        for b in range(n_f):
            turned[:, b * rows : (b + 1) * rows] = jnp.transpose(kv[b, which])

    def stacked(pair_block):
        return jnp.concatenate(
            [pair_block[:, h * HEAD_DIM : (h + 1) * HEAD_DIM] for h in range(PAIR)], axis=0
        )

    def scores_of(kv, query):
        def step(b, top):
            masked = jnp.concatenate([bias[span(b), :]] * PAIR, axis=1)
            scores = dot(piece(kv, 0, b), query, NT) * SCALE_LOG2 + masked
            s_buf[span(b), :] = scores
            return jnp.maximum(top, jnp.max(scores, axis=0, keepdims=True))

        return over_blocks(step, jnp.full((1, PAIR * rows), NEG, jnp.float32))

    def untangled(wide):
        return jnp.concatenate(
            [
                jnp.transpose(wide[:, h * rows : (h + 1) * rows])
                for h in range(PAIR)
            ],
            axis=1,
        ).astype(jnp.bfloat16)

    def lanes_of(pair):
        return pl.ds(pl.multiple_of(pair * pair_width, pair_width), pair_width)

    for copy in local:
        copy.wait()
    for copy in fwd:
        copy.wait_recv()
    make_bias(sg_fwd)
    turn(kv_fwd, 1)

    def forward_pair(pair, carry):
        query = stacked(q_buf[:, lanes_of(pair)])
        top = scores_of(kv_fwd, query)

        def step(b, sums):
            total, out = sums
            weights = jnp.exp2(s_buf[span(b), :] - top)
            total = total + jnp.sum(weights, axis=0, keepdims=True)
            out = out + dot(turned[:, span(b)], weights.astype(jnp.bfloat16))
            return total, out

        total, out = over_blocks(
            step,
            (
                jnp.zeros((1, PAIR * rows), jnp.float32),
                jnp.zeros((HEAD_DIM, PAIR * rows), jnp.float32),
            ),
        )
        o_buf[:, lanes_of(pair)] = untangled(out * (1.0 / total))
        return carry

    lax.fori_loop(0, pairs, forward_pair, 0)
    out_copy = pltpu.make_async_copy(o_buf, o_ref.at[0], local_sem.at[0])
    out_copy.start()

    for copy in second:
        copy.wait_recv()
    make_bias(sg_held)

    def columns_of(pair):
        return pl.ds(pl.multiple_of(pair * (PAIR * rows), PAIR * rows), PAIR * rows)

    def backward_pair(pair, carry):
        grad = stacked(g_buf[:, lanes_of(pair)])
        g_stack[columns_of(pair), :] = grad
        for step in range(n_t):
            query_copy(pair, step).wait_recv()
        query = stacked(hq_buf[pair])
        q_stack[columns_of(pair), :] = query
        top = scores_of(kv_held, query)

        def middle(b, sums):
            total, along = sums
            weights = jnp.exp2(s_buf[span(b), :] - top)
            prob_grad = dot(piece(kv_held, 1, b), grad, NT)
            s_buf[span(b), :] = weights
            p_buf[span(b), :] = prob_grad
            total = total + jnp.sum(weights, axis=0, keepdims=True)
            along = along + jnp.sum(weights * prob_grad, axis=0, keepdims=True)
            return total, along

        zero = jnp.zeros((1, PAIR * rows), jnp.float32)
        total, along = over_blocks(middle, (zero, zero))
        inverse = 1.0 / total
        delta = along * inverse

        def last(b, carry):
            probs = s_buf[span(b), :] * inverse
            score_grad = probs * (p_buf[span(b), :] - delta)
            p_low[span(b), columns_of(pair)] = probs.astype(jnp.bfloat16)
            d_low[span(b), columns_of(pair)] = score_grad.astype(jnp.bfloat16)
            return carry

        over_blocks(last, 0)
        return carry

    lax.fori_loop(0, pairs, backward_pair, 0)

    def rows_at(index):
        return pl.ds(pl.multiple_of(index * rows, rows), rows)

    def terms(index):
        key_part = dot(d_low[rows_at(index), :], q_stack[...])
        value_part = dot(p_low[rows_at(index), :], g_stack[...])
        return key_part, value_part

    reduce = []
    for step in range(1, n_f):
        to = at_f(step)
        key_part, value_part = terms(to)
        part_out[step - 1, 0] = key_part.astype(jnp.bfloat16)
        part_out[step - 1, 1] = value_part.astype(jnp.bfloat16)
        copy = remote(
            part_out.at[step - 1],
            part_in.at[step - 1],
            red_send.at[step - 1],
            red_recv.at[step - 1],
            (s, to, t),
        )
        copy.start()
        reduce.append(copy)

    turn(kv_held, 0)

    def query_pair(pair, carry):
        def step(b, query_sum):
            return query_sum + dot(turned[:, span(b)], d_low[span(b), columns_of(pair)])

        query_sum = over_blocks(step, jnp.zeros((HEAD_DIM, PAIR * rows), jnp.float32))
        dq_buf[:, lanes_of(pair)] = untangled(query_sum * SCALE)
        return carry

    lax.fori_loop(0, pairs, query_pair, 0)
    query_grad_copy = pltpu.make_async_copy(dq_buf, dq_ref.at[0], local_sem.at[1])
    query_grad_copy.start()

    key_sum, value_sum = terms(f)
    for step in range(1, n_f):
        reduce[step - 1].wait_recv()
        key_sum = key_sum + part_in[step - 1, 0].astype(jnp.float32)
        value_sum = value_sum + part_in[step - 1, 1].astype(jnp.float32)
    dk_buf[...] = (key_sum * SCALE).astype(jnp.bfloat16)
    dv_buf[...] = value_sum.astype(jnp.bfloat16)
    last_copies = [
        pltpu.make_async_copy(dk_buf, dk_ref.at[0], local_sem.at[2]),
        pltpu.make_async_copy(dv_buf, dv_ref.at[0], local_sem.at[3]),
    ]
    for copy in last_copies:
        copy.start()
    for copy in first + fwd + second + reduce:
        copy.wait_send()
    for pair in range(pairs):
        for step in range(n_t):
            query_copy(pair, step).wait_send()
    for copy in [out_copy, query_grad_copy] + last_copies:
        copy.wait()


def hand_over(*refs):
    count = len(refs) // 2
    sems = refs[-1]
    copies = [
        pltpu.make_async_copy(refs[i], refs[count + i], sems.at[i]) for i in range(count)
    ]
    for copy in copies:
        copy.start()
    for copy in copies:
        copy.wait()


def local(sizes, *arrays):
    n_s, n_f, n_t = sizes
    queries, key_rows = arrays[0], arrays[1]
    rows, width = queries.shape[1], queries.shape[2]
    pairs = width // (PAIR * HEAD_DIM)
    seq = n_f * rows
    low, full = jnp.bfloat16, jnp.float32
    dma = pltpu.SemaphoreType.DMA
    anywhere = pl.BlockSpec(memory_space=pl.ANY)
    elements = rows * (width // HEAD_DIM) * seq
    results = pl.pallas_call(
        functools.partial(kernel, n_s, n_f, n_t),
        out_shape=[
            jax.ShapeDtypeStruct(queries.shape, low),
            jax.ShapeDtypeStruct(queries.shape, low),
            jax.ShapeDtypeStruct(key_rows.shape, low),
            jax.ShapeDtypeStruct(key_rows.shape, low),
        ],
        in_specs=[anywhere] * 9,
        out_specs=[anywhere] * 4,
        scratch_shapes=[
            pltpu.VMEM((rows, width), low),
            pltpu.VMEM((rows, width), low),
            pltpu.VMEM((n_f, 2, rows, HEAD_DIM), low),
            pltpu.VMEM((n_f, 1, rows), jnp.int32),
            pltpu.VMEM((pairs, rows, PAIR * HEAD_DIM), low),
            pltpu.VMEM((n_f, 2, rows, HEAD_DIM), low),
            pltpu.VMEM((n_f, 1, rows), jnp.int32),
            pltpu.VMEM((seq, rows), full),
            pltpu.VMEM((HEAD_DIM, seq), low),
            pltpu.VMEM((seq, PAIR * rows), full),
            pltpu.VMEM((seq, PAIR * rows), full),
            pltpu.VMEM((seq, pairs * PAIR * rows), low),
            pltpu.VMEM((seq, pairs * PAIR * rows), low),
            pltpu.VMEM((pairs * PAIR * rows, HEAD_DIM), low),
            pltpu.VMEM((pairs * PAIR * rows, HEAD_DIM), low),
            pltpu.VMEM((n_f - 1, 2, rows, HEAD_DIM), low),
            pltpu.VMEM((n_f - 1, 2, rows, HEAD_DIM), low),
            pltpu.VMEM((rows, width), low),
            pltpu.VMEM((rows, width), low),
            pltpu.VMEM((rows, HEAD_DIM), low),
            pltpu.VMEM((rows, HEAD_DIM), low),
            dma((5,)),
            dma((3 * (n_f - 1),)),
            dma((3 * (n_f - 1),)),
            dma((2 * n_t + 1,)),
            dma((2 * n_t + 1,)),
            dma((2 * (n_f - 1),)),
            dma((2 * (n_f - 1),)),
            dma((pairs, n_t)),
            dma((pairs, n_t)),
            dma((n_f - 1,)),
            dma((n_f - 1,)),
        ],
        compiler_params=pltpu.CompilerParams(
            collective_id=0, has_side_effects=True, vmem_limit_bytes=VMEM_BYTES
        ),
        cost_estimate=pl.CostEstimate(
            flops=14 * elements * HEAD_DIM,
            bytes_accessed=6 * rows * width * 2,
            transcendentals=2 * elements,
        ),
        name="tick",
    )(*arrays)
    return pl.pallas_call(
        hand_over,
        out_shape=[jax.ShapeDtypeStruct(result.shape, low) for result in results],
        in_specs=[anywhere] * len(results),
        out_specs=[anywhere] * len(results),
        scratch_shapes=[dma((len(results),))],
        compiler_params=pltpu.CompilerParams(vmem_limit_bytes=VMEM_BYTES),
        name="hand_over",
    )(*results)


def solution(mesh):
    sizes = (mesh.shape["section"], mesh.shape["fsdp"], mesh.shape["tp"])
    by_head = P("section", "fsdp", "tp")
    by_row = P("section", ("fsdp", "tp"), None)
    ids = P("section", "fsdp")
    return jax.shard_map(
        functools.partial(local, sizes),
        mesh=mesh,
        in_specs=(by_head, by_head, by_head, ids, by_row, by_row, by_row, ids, by_head),
        out_specs=(by_head,) * 4,
        check_vma=False,
    )
```

```python
import functools
import math

import jax
import jax.numpy as jnp
from jax import lax
from jax.experimental import pallas as pl
from jax.experimental.pallas import tpu as pltpu
from jax.sharding import PartitionSpec as P

HEAD_DIM = 128
PAIR = 2
LOW = 2
NEG = -1e30
SCALE = 1.0 / math.sqrt(HEAD_DIM)
SCALE_LOG2 = SCALE * math.log2(math.e)
MESH = pl.DeviceIdType.MESH
VMEM_BYTES = 63 * 1024 * 1024

NT = (((1,), (1,)), ((), ()))


def dot(left, right, dims=(((1,), (0,)), ((), ()))):
    return lax.dot_general(left, right, dims, preferred_element_type=jnp.float32)


def kernel(
    n_s,
    n_f,
    n_t,
    q_ref,
    k_ref,
    v_ref,
    sg_ref,
    hq_ref,
    hk_ref,
    hv_ref,
    hs_ref,
    do_ref,
    o_ref,
    dq_ref,
    dk_ref,
    dv_ref,
    q_buf,
    g_buf,
    kv_fwd,
    sg_fwd,
    hq_buf,
    kv_held,
    sg_held,
    bias,
    turned,
    s_buf,
    p_buf,
    p_low,
    d_low,
    q_stack,
    g_stack,
    part_out,
    part_in,
    o_buf,
    dq_buf,
    dk_buf,
    dv_buf,
    local_sem,
    fwd_send,
    fwd_recv,
    one_send,
    one_recv,
    two_send,
    two_recv,
    hq_send,
    hq_recv,
    ids_send,
    ids_recv,
    on_send,
    on_recv,
    red_send,
    red_recv,
):
    rows = q_ref.shape[1]
    part_rows = hq_ref.shape[1]
    width = q_ref.shape[2]
    pair_width = PAIR * HEAD_DIM
    pairs = width // pair_width
    seq = n_f * rows
    block = min(512, seq)
    blocks = seq // block

    s, f, t = lax.axis_index("section"), lax.axis_index("fsdp"), lax.axis_index("tp")
    mirror = n_s - 1 - s

    def at_f(step):
        return lax.rem(f + step, n_f)

    high, low_index = f // LOW, f % LOW
    n_high = n_f // LOW
    sibling = high * LOW + (LOW - 1 - low_index)

    def at_high(step):
        return lax.rem(high + step, n_high) * LOW + low_index

    def from_high(step):
        return lax.rem(high + n_high - step, n_high) * LOW + low_index

    def beside(index):
        return index - low_index + (LOW - 1 - low_index)

    def at_t(step):
        return lax.rem(t + step, n_t)

    local = [
        pltpu.make_async_copy(k_ref.at[0], kv_fwd.at[f, 0], local_sem.at[0]),
        pltpu.make_async_copy(v_ref.at[0], kv_fwd.at[f, 1], local_sem.at[1]),
        pltpu.make_async_copy(sg_ref, sg_fwd.at[f], local_sem.at[2]),
        pltpu.make_async_copy(q_ref.at[0], q_buf, local_sem.at[3]),
        pltpu.make_async_copy(do_ref.at[0], g_buf, local_sem.at[4]),
    ]
    for copy in local:
        copy.start()

    barrier = pltpu.get_barrier_semaphore()
    for step in range(n_t):
        pl.semaphore_signal(
            barrier, inc=1, device_id=(mirror, f, at_t(step)), device_id_type=MESH
        )
    for step in range(1, n_f):
        pl.semaphore_signal(barrier, inc=1, device_id=(s, at_f(step), t), device_id_type=MESH)
    pl.semaphore_wait(barrier, n_t + n_f - 1)

    def remote(src, dst, send_sem, recv_sem, device):
        return pltpu.make_async_remote_copy(
            src_ref=src,
            dst_ref=dst,
            send_sem=send_sem,
            recv_sem=recv_sem,
            device_id=device,
            device_id_type=MESH,
        )

    own_rows = pl.ds(pl.multiple_of(t * part_rows, part_rows), part_rows)

    first = []
    for step in range(n_t):
        to = at_t(step)
        columns = pl.ds(pl.multiple_of(to * HEAD_DIM, HEAD_DIM), HEAD_DIM)
        for which, held in enumerate((hk_ref, hv_ref)):
            first.append(
                remote(
                    held.at[0, :, columns],
                    kv_held.at[f, which, own_rows, :],
                    one_send.at[2 * step + which],
                    one_recv.at[2 * step + which],
                    (mirror, f, to),
                )
            )
    first.append(
        remote(
            hs_ref,
            sg_held.at[f],
            one_send.at[2 * n_t],
            one_recv.at[2 * n_t],
            (mirror, f, t),
        )
    )
    for copy in first:
        copy.start()

    ids_fwd = [
        remote(
            sg_ref,
            sg_fwd.at[f],
            ids_send.at[step - 1],
            ids_recv.at[step - 1],
            (s, at_f(step), t),
        )
        for step in range(1, n_f)
    ]
    fwd = []
    for step in range(n_high):
        device = (s, sibling if step == 0 else at_high(step), t)
        for which, src in enumerate((k_ref, v_ref)):
            at = 2 * step + which
            fwd.append(
                remote(
                    src.at[0], kv_fwd.at[f, which], fwd_send.at[at], fwd_recv.at[at], device
                )
            )
    for copy in fwd[2:] + fwd[:2] + ids_fwd:
        copy.start()

    def passed_on(kv, send_sem, recv_sem):
        return [
            remote(
                kv.at[from_high(step)],
                kv.at[from_high(step)],
                send_sem.at[step - 1],
                recv_sem.at[step - 1],
                (s, sibling, t),
            )
            for step in range(1, n_high)
        ]

    def query_copy(pair, step):
        to = at_t(step)
        columns = pl.ds(
            pl.multiple_of(to * width + pair * pair_width, pair_width), pair_width
        )
        return remote(
            hq_ref.at[0, :, columns],
            hq_buf.at[pair, own_rows, :],
            hq_send.at[pair, step],
            hq_recv.at[pair, step],
            (mirror, f, to),
        )

    for pair in range(pairs):
        for step in range(n_t):
            query_copy(pair, step).start()

    for copy in first:
        copy.wait_recv()
    second = []
    for step in range(n_high):
        device = (s, sibling if step == 0 else at_high(step), t)
        second.append(
            remote(kv_held.at[f], kv_held.at[f], two_send.at[step], two_recv.at[step], device)
        )
    ids_held = [
        remote(
            sg_held.at[f],
            sg_held.at[f],
            ids_send.at[n_f - 2 + step],
            ids_recv.at[n_f - 2 + step],
            (s, at_f(step), t),
        )
        for step in range(1, n_f)
    ]
    for copy in second[1:] + second[:1] + ids_held:
        copy.start()

    for copy in fwd[2:]:
        copy.wait_recv()
    fwd_on = passed_on(kv_fwd, on_send.at[0], on_recv.at[0])
    for copy in fwd_on:
        copy.start()

    def make_bias(ids):
        own = ids[f]
        for b in range(n_f):
            key_ids = jnp.transpose(jnp.broadcast_to(ids[b], (rows, rows)))
            key_pos = b * rows + lax.broadcasted_iota(jnp.int32, (rows, rows), 0)
            own_pos = f * rows + lax.broadcasted_iota(jnp.int32, (rows, rows), 1)
            seen = (key_pos <= own_pos) & (key_ids == own)
            bias[b * rows : (b + 1) * rows, :] = jnp.where(seen, 0.0, NEG)

    def over_blocks(step, start):
        if blocks == 1:
            return step(0, start)
        return lax.fori_loop(0, blocks, step, start)

    def span(b):
        if blocks == 1:
            return pl.ds(0, block)
        return pl.ds(pl.multiple_of(b * block, block), block)

    def piece(kv, which, b):
        per = block // rows
        if blocks == 1:
            part = kv[:, which]
        else:
            part = kv[pl.ds(b * per, per), which]
        return part.reshape(block, HEAD_DIM)

    def turn(kv, which):
        for b in range(n_f):
            turned[:, b * rows : (b + 1) * rows] = jnp.transpose(kv[b, which])

    def stacked(pair_block):
        return jnp.concatenate(
            [pair_block[:, h * HEAD_DIM : (h + 1) * HEAD_DIM] for h in range(PAIR)], axis=0
        )

    def scores_of(kv, query):
        def step(b, top):
            masked = jnp.concatenate([bias[span(b), :]] * PAIR, axis=1)
            scores = dot(piece(kv, 0, b), query, NT) * SCALE_LOG2 + masked
            s_buf[span(b), :] = scores
            return jnp.maximum(top, jnp.max(scores, axis=0, keepdims=True))

        return over_blocks(step, jnp.full((1, PAIR * rows), NEG, jnp.float32))

    def untangled(wide):
        return jnp.concatenate(
            [
                jnp.transpose(wide[:, h * rows : (h + 1) * rows])
                for h in range(PAIR)
            ],
            axis=1,
        ).astype(jnp.bfloat16)

    def lanes_of(pair):
        return pl.ds(pl.multiple_of(pair * pair_width, pair_width), pair_width)

    for copy in local:
        copy.wait()
    for copy in ids_fwd:
        copy.wait_recv()
    make_bias(sg_fwd)
    for copy in fwd[:2] + fwd_on:
        copy.wait_recv()
    turn(kv_fwd, 1)

    def forward_pair(pair, carry):
        query = stacked(q_buf[:, lanes_of(pair)])
        top = scores_of(kv_fwd, query)

        def step(b, sums):
            total, out = sums
            weights = jnp.exp2(s_buf[span(b), :] - top)
            total = total + jnp.sum(weights, axis=0, keepdims=True)
            out = out + dot(turned[:, span(b)], weights.astype(jnp.bfloat16))
            return total, out

        total, out = over_blocks(
            step,
            (
                jnp.zeros((1, PAIR * rows), jnp.float32),
                jnp.zeros((HEAD_DIM, PAIR * rows), jnp.float32),
            ),
        )
        o_buf[:, lanes_of(pair)] = untangled(out * (1.0 / total))
        return carry

    lax.fori_loop(0, pairs // 2, forward_pair, 0)
    for copy in second[1:]:
        copy.wait_recv()
    held_on = passed_on(kv_held, on_send.at[1], on_recv.at[1])
    for copy in held_on:
        copy.start()
    lax.fori_loop(pairs // 2, pairs, forward_pair, 0)
    out_copy = pltpu.make_async_copy(o_buf, o_ref.at[0], local_sem.at[0])
    out_copy.start()

    for copy in ids_held:
        copy.wait_recv()
    make_bias(sg_held)
    for copy in second[:1] + held_on:
        copy.wait_recv()

    def columns_of(pair):
        return pl.ds(pl.multiple_of(pair * (PAIR * rows), PAIR * rows), PAIR * rows)

    def backward_pair(pair, carry):
        grad = stacked(g_buf[:, lanes_of(pair)])
        g_stack[columns_of(pair), :] = grad
        for step in range(n_t):
            query_copy(pair, step).wait_recv()
        query = stacked(hq_buf[pair])
        q_stack[columns_of(pair), :] = query
        top = scores_of(kv_held, query)

        def middle(b, sums):
            total, along = sums
            weights = jnp.exp2(s_buf[span(b), :] - top)
            prob_grad = dot(piece(kv_held, 1, b), grad, NT)
            s_buf[span(b), :] = weights
            p_buf[span(b), :] = prob_grad
            total = total + jnp.sum(weights, axis=0, keepdims=True)
            along = along + jnp.sum(weights * prob_grad, axis=0, keepdims=True)
            return total, along

        zero = jnp.zeros((1, PAIR * rows), jnp.float32)
        total, along = over_blocks(middle, (zero, zero))
        inverse = 1.0 / total
        delta = along * inverse

        def last(b, carry):
            probs = s_buf[span(b), :] * inverse
            score_grad = probs * (p_buf[span(b), :] - delta)
            p_low[span(b), columns_of(pair)] = probs.astype(jnp.bfloat16)
            d_low[span(b), columns_of(pair)] = score_grad.astype(jnp.bfloat16)
            return carry

        over_blocks(last, 0)
        return carry

    lax.fori_loop(0, pairs, backward_pair, 0)

    def rows_at(index):
        return pl.ds(pl.multiple_of(index * rows, rows), rows)

    def terms(index):
        key_part = dot(d_low[rows_at(index), :], q_stack[...])
        value_part = dot(p_low[rows_at(index), :], g_stack[...])
        return key_part, value_part

    def reduce_copy(at, device):
        return remote(
            part_out.at[at], part_in.at[at], red_send.at[at], red_recv.at[at], device
        )

    def put(at, parts):
        for which in range(2):
            part_out[at, which] = parts[which].astype(jnp.bfloat16)

    def taken(at, parts):
        return [parts[which] + part_in[at, which].astype(jnp.float32) for which in range(2)]

    others = n_high - 1
    reduce = []
    for step in range(1, n_high):
        put(step - 1, terms(beside(at_high(step))))
        reduce.append(reduce_copy(step - 1, (s, sibling, t)))
        reduce[-1].start()
    for_others = [terms(at_high(step)) for step in range(1, n_high)]
    put(2 * others, terms(sibling))
    reduce_side = reduce_copy(2 * others, (s, sibling, t))
    reduce_side.start()
    reduce_across = []
    for step in range(1, n_high):
        reduce[step - 1].wait_recv()
        put(others + step - 1, taken(step - 1, for_others[step - 1]))
        reduce_across.append(reduce_copy(others + step - 1, (s, at_high(step), t)))
        reduce_across[-1].start()

    turn(kv_held, 0)

    def query_pair(pair, carry):
        def step(b, query_sum):
            return query_sum + dot(turned[:, span(b)], d_low[span(b), columns_of(pair)])

        query_sum = over_blocks(step, jnp.zeros((HEAD_DIM, PAIR * rows), jnp.float32))
        dq_buf[:, lanes_of(pair)] = untangled(query_sum * SCALE)
        return carry

    lax.fori_loop(0, pairs, query_pair, 0)
    query_grad_copy = pltpu.make_async_copy(dq_buf, dq_ref.at[0], local_sem.at[1])
    query_grad_copy.start()

    sums = terms(f)
    reduce_side.wait_recv()
    sums = taken(2 * others, sums)
    for step in range(1, n_high):
        reduce_across[step - 1].wait_recv()
        sums = taken(others + step - 1, sums)
    key_sum, value_sum = sums
    dk_buf[...] = (key_sum * SCALE).astype(jnp.bfloat16)
    dv_buf[...] = value_sum.astype(jnp.bfloat16)
    last_copies = [
        pltpu.make_async_copy(dk_buf, dk_ref.at[0], local_sem.at[2]),
        pltpu.make_async_copy(dv_buf, dv_ref.at[0], local_sem.at[3]),
    ]
    for copy in last_copies:
        copy.start()
    for copy in (
        first + fwd + fwd_on + second + held_on + ids_fwd + ids_held
        + reduce + reduce_across + [reduce_side]
    ):
        copy.wait_send()
    for pair in range(pairs):
        for step in range(n_t):
            query_copy(pair, step).wait_send()
    for copy in [out_copy, query_grad_copy] + last_copies:
        copy.wait()


def hand_over(*refs):
    count = (len(refs) - 2) // 3
    sources, results, held = refs[:count], refs[count : 2 * count], refs[2 * count : 3 * count]
    in_sem, out_sem = refs[3 * count :]
    into = [pltpu.make_async_copy(sources[i], held[i], in_sem.at[i]) for i in range(count)]
    out = [pltpu.make_async_copy(held[i], results[i], out_sem.at[i]) for i in range(count)]
    for copy in into:
        copy.start()
    for i in range(count):
        into[i].wait()
        out[i].start()
    for copy in out:
        copy.wait()


def local(sizes, *arrays):
    n_s, n_f, n_t = sizes
    queries, key_rows = arrays[0], arrays[1]
    rows, width = queries.shape[1], queries.shape[2]
    pairs = width // (PAIR * HEAD_DIM)
    seq = n_f * rows
    low, full = jnp.bfloat16, jnp.float32
    dma = pltpu.SemaphoreType.DMA
    anywhere = pl.BlockSpec(memory_space=pl.ANY)
    elements = rows * (width // HEAD_DIM) * seq
    results = pl.pallas_call(
        functools.partial(kernel, n_s, n_f, n_t),
        out_shape=[
            jax.ShapeDtypeStruct(queries.shape, low),
            jax.ShapeDtypeStruct(queries.shape, low),
            jax.ShapeDtypeStruct(key_rows.shape, low),
            jax.ShapeDtypeStruct(key_rows.shape, low),
        ],
        in_specs=[anywhere] * 9,
        out_specs=[anywhere] * 4,
        scratch_shapes=[
            pltpu.VMEM((rows, width), low),
            pltpu.VMEM((rows, width), low),
            pltpu.VMEM((n_f, 2, rows, HEAD_DIM), low),
            pltpu.VMEM((n_f, 1, rows), jnp.int32),
            pltpu.VMEM((pairs, rows, PAIR * HEAD_DIM), low),
            pltpu.VMEM((n_f, 2, rows, HEAD_DIM), low),
            pltpu.VMEM((n_f, 1, rows), jnp.int32),
            pltpu.VMEM((seq, rows), full),
            pltpu.VMEM((HEAD_DIM, seq), low),
            pltpu.VMEM((seq, PAIR * rows), full),
            pltpu.VMEM((seq, PAIR * rows), full),
            pltpu.VMEM((seq, pairs * PAIR * rows), low),
            pltpu.VMEM((seq, pairs * PAIR * rows), low),
            pltpu.VMEM((pairs * PAIR * rows, HEAD_DIM), low),
            pltpu.VMEM((pairs * PAIR * rows, HEAD_DIM), low),
            pltpu.VMEM((n_f - 1, 2, rows, HEAD_DIM), low),
            pltpu.VMEM((n_f - 1, 2, rows, HEAD_DIM), low),
            pltpu.VMEM((rows, width), low),
            pltpu.VMEM((rows, width), low),
            pltpu.VMEM((rows, HEAD_DIM), low),
            pltpu.VMEM((rows, HEAD_DIM), low),
            dma((5,)),
            dma((n_f,)),
            dma((n_f,)),
            dma((2 * n_t + 1,)),
            dma((2 * n_t + 1,)),
            dma((n_f // LOW,)),
            dma((n_f // LOW,)),
            dma((pairs, n_t)),
            dma((pairs, n_t)),
            dma((2 * (n_f - 1),)),
            dma((2 * (n_f - 1),)),
            dma((2, n_f // LOW - 1)),
            dma((2, n_f // LOW - 1)),
            dma((n_f - 1,)),
            dma((n_f - 1,)),
        ],
        compiler_params=pltpu.CompilerParams(
            collective_id=0, has_side_effects=True, vmem_limit_bytes=VMEM_BYTES
        ),
        cost_estimate=pl.CostEstimate(
            flops=14 * elements * HEAD_DIM,
            bytes_accessed=6 * rows * width * 2,
            transcendentals=2 * elements,
        ),
        name="tick",
    )(*arrays)
    return pl.pallas_call(
        hand_over,
        out_shape=[jax.ShapeDtypeStruct(result.shape, low) for result in results],
        in_specs=[anywhere] * len(results),
        out_specs=[anywhere] * len(results),
        scratch_shapes=[pltpu.VMEM(result.shape, low) for result in results]
        + [dma((len(results),)), dma((len(results),))],
        compiler_params=pltpu.CompilerParams(vmem_limit_bytes=VMEM_BYTES),
        name="hand_over",
    )(*results)


def solution(mesh):
    sizes = (mesh.shape["section"], mesh.shape["fsdp"], mesh.shape["tp"])
    by_head = P("section", "fsdp", "tp")
    by_row = P("section", ("fsdp", "tp"), None)
    ids = P("section", "fsdp")
    return jax.shard_map(
        functools.partial(local, sizes),
        mesh=mesh,
        in_specs=(by_head, by_head, by_head, ids, by_row, by_row, by_row, ids, by_head),
        out_specs=(by_head,) * 4,
        check_vma=False,
    )
```

```python
import functools
import math

import jax
import jax.numpy as jnp
from jax import lax
from jax.experimental import pallas as pl
from jax.experimental.pallas import tpu as pltpu
from jax.sharding import PartitionSpec as P

HEAD_DIM = 128
PAIR = 4
NEG = -1e30
SCALE = 1.0 / math.sqrt(HEAD_DIM)
SCALE_LOG2 = SCALE * math.log2(math.e)
MESH = pl.DeviceIdType.MESH
VMEM_BYTES = 63 * 1024 * 1024

NT = (((1,), (1,)), ((), ()))


def dot(left, right, dims=(((1,), (0,)), ((), ()))):
    return lax.dot_general(left, right, dims, preferred_element_type=jnp.float32)


def kernel(
    n_s,
    n_f,
    n_t,
    q_ref,
    k_ref,
    v_ref,
    sg_ref,
    hq_ref,
    hk_ref,
    hv_ref,
    hs_ref,
    do_ref,
    o_ref,
    dq_ref,
    dk_ref,
    dv_ref,
    q_buf,
    g_buf,
    kv_fwd,
    sg_fwd,
    hq_buf,
    kv_held,
    sg_held,
    bias,
    bias_held,
    turned,
    turned_held,
    s_buf,
    p_buf,
    p_low,
    d_low,
    q_stack,
    g_stack,
    part_out,
    part_in,
    o_buf,
    dq_buf,
    dk_buf,
    dv_buf,
    local_sem,
    fwd_send,
    fwd_recv,
    one_send,
    one_recv,
    two_send,
    two_recv,
    hq_send,
    hq_recv,
    red_send,
    red_recv,
):
    rows = q_ref.shape[1]
    part_rows = hq_ref.shape[1]
    width = q_ref.shape[2]
    pair_width = PAIR * HEAD_DIM
    pairs = width // pair_width
    seq = n_f * rows
    block = min(512, seq)
    blocks = seq // block

    s, f, t = lax.axis_index("section"), lax.axis_index("fsdp"), lax.axis_index("tp")
    mirror = n_s - 1 - s

    def at_f(step):
        return lax.rem(f + step, n_f)

    def at_t(step):
        return lax.rem(t + step, n_t)

    local = [
        pltpu.make_async_copy(k_ref.at[0], kv_fwd.at[f, 0], local_sem.at[0]),
        pltpu.make_async_copy(v_ref.at[0], kv_fwd.at[f, 1], local_sem.at[1]),
        pltpu.make_async_copy(sg_ref, sg_fwd.at[f], local_sem.at[2]),
        pltpu.make_async_copy(q_ref.at[0], q_buf, local_sem.at[3]),
        pltpu.make_async_copy(do_ref.at[0], g_buf, local_sem.at[4]),
    ]
    for copy in local:
        copy.start()

    barrier = pltpu.get_barrier_semaphore()
    for step in range(n_t):
        pl.semaphore_signal(
            barrier, inc=1, device_id=(mirror, f, at_t(step)), device_id_type=MESH
        )
    for step in range(1, n_f):
        pl.semaphore_signal(barrier, inc=1, device_id=(s, at_f(step), t), device_id_type=MESH)
    pl.semaphore_wait(barrier, n_t + n_f - 1)

    def remote(src, dst, send_sem, recv_sem, device):
        return pltpu.make_async_remote_copy(
            src_ref=src,
            dst_ref=dst,
            send_sem=send_sem,
            recv_sem=recv_sem,
            device_id=device,
            device_id_type=MESH,
        )

    own_rows = pl.ds(pl.multiple_of(t * part_rows, part_rows), part_rows)

    first = []
    for step in range(n_t):
        to = at_t(step)
        columns = pl.ds(pl.multiple_of(to * HEAD_DIM, HEAD_DIM), HEAD_DIM)
        for which, held in enumerate((hk_ref, hv_ref)):
            first.append(
                remote(
                    held.at[0, :, columns],
                    kv_held.at[f, which, own_rows, :],
                    one_send.at[2 * step + which],
                    one_recv.at[2 * step + which],
                    (mirror, f, to),
                )
            )
    first.append(
        remote(
            hs_ref,
            sg_held.at[f],
            one_send.at[2 * n_t],
            one_recv.at[2 * n_t],
            (mirror, f, t),
        )
    )
    for copy in first:
        copy.start()

    fwd = []
    for step in range(1, n_f):
        device = (s, at_f(step), t)
        at = 3 * (step - 1)
        for which, src in enumerate((k_ref.at[0], v_ref.at[0], sg_ref)):
            dst = sg_fwd.at[f] if which == 2 else kv_fwd.at[f, which]
            fwd.append(
                remote(src, dst, fwd_send.at[at + which], fwd_recv.at[at + which], device)
            )
    for copy in fwd:
        copy.start()

    def query_copy(pair, step):
        to = at_t(step)
        columns = pl.ds(
            pl.multiple_of(to * width + pair * pair_width, pair_width), pair_width
        )
        return remote(
            hq_ref.at[0, :, columns],
            hq_buf.at[pair, own_rows, :],
            hq_send.at[pair, step],
            hq_recv.at[pair, step],
            (mirror, f, to),
        )

    for pair in range(pairs):
        for step in range(n_t):
            query_copy(pair, step).start()

    for copy in first:
        copy.wait_recv()
    second = []
    for step in range(1, n_f):
        device = (s, at_f(step), t)
        at = 2 * (step - 1)
        second.append(
            remote(
                kv_held.at[f], kv_held.at[f], two_send.at[at], two_recv.at[at], device
            )
        )
        second.append(
            remote(
                sg_held.at[f],
                sg_held.at[f],
                two_send.at[at + 1],
                two_recv.at[at + 1],
                device,
            )
        )
    for copy in second:
        copy.start()

    def make_bias(ids, bias):
        own = ids[f]
        for b in range(n_f):
            key_ids = jnp.transpose(jnp.broadcast_to(ids[b], (rows, rows)))
            key_pos = b * rows + lax.broadcasted_iota(jnp.int32, (rows, rows), 0)
            own_pos = f * rows + lax.broadcasted_iota(jnp.int32, (rows, rows), 1)
            seen = (key_pos <= own_pos) & (key_ids == own)
            bias[b * rows : (b + 1) * rows, :] = jnp.where(seen, 0.0, NEG)

    def over_blocks(step, start):
        if blocks == 1:
            return step(0, start)
        return lax.fori_loop(0, blocks, step, start)

    def span(b):
        if blocks == 1:
            return pl.ds(0, block)
        return pl.ds(pl.multiple_of(b * block, block), block)

    def piece(kv, which, b):
        per = block // rows
        if blocks == 1:
            part = kv[:, which]
        else:
            part = kv[pl.ds(b * per, per), which]
        return part.reshape(block, HEAD_DIM)

    def turn(kv, which, turned):
        for b in range(n_f):
            turned[:, b * rows : (b + 1) * rows] = jnp.transpose(kv[b, which])

    def stacked(pair_block):
        return jnp.concatenate(
            [pair_block[:, h * HEAD_DIM : (h + 1) * HEAD_DIM] for h in range(PAIR)], axis=0
        )

    def scores_of(kv, query, bias):
        def step(b, top):
            masked = jnp.concatenate([bias[span(b), :]] * PAIR, axis=1)
            scores = dot(piece(kv, 0, b), query, NT) * SCALE_LOG2 + masked
            s_buf[span(b), :] = scores
            return jnp.maximum(top, jnp.max(scores, axis=0, keepdims=True))

        return over_blocks(step, jnp.full((1, PAIR * rows), NEG, jnp.float32))

    def untangled(wide):
        return jnp.concatenate(
            [
                jnp.transpose(wide[:, h * rows : (h + 1) * rows])
                for h in range(PAIR)
            ],
            axis=1,
        ).astype(jnp.bfloat16)

    def lanes_of(pair):
        return pl.ds(pl.multiple_of(pair * pair_width, pair_width), pair_width)

    for copy in local:
        copy.wait()
    for copy in fwd:
        copy.wait_recv()
    make_bias(sg_fwd, bias)
    turn(kv_fwd, 1, turned)

    def forward_pair(pair, carry):
        query = stacked(q_buf[:, lanes_of(pair)])
        top = scores_of(kv_fwd, query, bias)

        def step(b, sums):
            total, out = sums
            weights = jnp.exp2(s_buf[span(b), :] - top)
            total = total + jnp.sum(weights, axis=0, keepdims=True)
            out = out + dot(turned[:, span(b)], weights.astype(jnp.bfloat16))
            return total, out

        total, out = over_blocks(
            step,
            (
                jnp.zeros((1, PAIR * rows), jnp.float32),
                jnp.zeros((HEAD_DIM, PAIR * rows), jnp.float32),
            ),
        )
        o_buf[:, lanes_of(pair)] = untangled(out * (1.0 / total))
        return carry

    lax.fori_loop(0, pairs // 2, forward_pair, 0)

    for copy in second:
        copy.wait_recv()
    make_bias(sg_held, bias_held)

    def columns_of(pair):
        return pl.ds(pl.multiple_of(pair * (PAIR * rows), PAIR * rows), PAIR * rows)

    def backward_pair(pair, carry):
        grad = stacked(g_buf[:, lanes_of(pair)])
        g_stack[columns_of(pair), :] = grad
        for step in range(n_t):
            query_copy(pair, step).wait_recv()
        query = stacked(hq_buf[pair])
        q_stack[columns_of(pair), :] = query
        top = scores_of(kv_held, query, bias_held)

        def middle(b, sums):
            total, along = sums
            weights = jnp.exp2(s_buf[span(b), :] - top)
            prob_grad = dot(piece(kv_held, 1, b), grad, NT)
            s_buf[span(b), :] = weights
            p_buf[span(b), :] = prob_grad
            total = total + jnp.sum(weights, axis=0, keepdims=True)
            along = along + jnp.sum(weights * prob_grad, axis=0, keepdims=True)
            return total, along

        zero = jnp.zeros((1, PAIR * rows), jnp.float32)
        total, along = over_blocks(middle, (zero, zero))
        inverse = 1.0 / total
        delta = along * inverse

        def last(b, carry):
            probs = s_buf[span(b), :] * inverse
            score_grad = probs * (p_buf[span(b), :] - delta)
            p_low[span(b), columns_of(pair)] = probs.astype(jnp.bfloat16)
            d_low[span(b), columns_of(pair)] = score_grad.astype(jnp.bfloat16)
            return carry

        over_blocks(last, 0)
        return carry

    lax.fori_loop(0, pairs, backward_pair, 0)

    def rows_at(index):
        return pl.ds(pl.multiple_of(index * rows, rows), rows)

    def terms(index):
        key_part = dot(d_low[rows_at(index), :], q_stack[...])
        value_part = dot(p_low[rows_at(index), :], g_stack[...])
        return key_part, value_part

    reduce = []
    for step in range(1, n_f):
        to = at_f(step)
        key_part, value_part = terms(to)
        part_out[step - 1, 0] = key_part.astype(jnp.bfloat16)
        part_out[step - 1, 1] = value_part.astype(jnp.bfloat16)
        copy = remote(
            part_out.at[step - 1],
            part_in.at[step - 1],
            red_send.at[step - 1],
            red_recv.at[step - 1],
            (s, to, t),
        )
        copy.start()
        reduce.append(copy)

    turn(kv_held, 0, turned_held)

    def query_pair(pair, carry):
        def step(b, query_sum):
            return query_sum + dot(turned_held[:, span(b)], d_low[span(b), columns_of(pair)])

        query_sum = over_blocks(step, jnp.zeros((HEAD_DIM, PAIR * rows), jnp.float32))
        dq_buf[:, lanes_of(pair)] = untangled(query_sum * SCALE)
        return carry

    lax.fori_loop(0, pairs, query_pair, 0)
    query_grad_copy = pltpu.make_async_copy(dq_buf, dq_ref.at[0], local_sem.at[1])
    query_grad_copy.start()
    lax.fori_loop(pairs // 2, pairs, forward_pair, 0)
    out_copy = pltpu.make_async_copy(o_buf, o_ref.at[0], local_sem.at[0])
    out_copy.start()

    key_sum, value_sum = terms(f)
    for step in range(1, n_f):
        reduce[step - 1].wait_recv()
        key_sum = key_sum + part_in[step - 1, 0].astype(jnp.float32)
        value_sum = value_sum + part_in[step - 1, 1].astype(jnp.float32)
    dk_buf[...] = (key_sum * SCALE).astype(jnp.bfloat16)
    dv_buf[...] = value_sum.astype(jnp.bfloat16)
    last_copies = [
        pltpu.make_async_copy(dk_buf, dk_ref.at[0], local_sem.at[2]),
        pltpu.make_async_copy(dv_buf, dv_ref.at[0], local_sem.at[3]),
    ]
    for copy in last_copies:
        copy.start()
    for copy in first + fwd + second + reduce:
        copy.wait_send()
    for pair in range(pairs):
        for step in range(n_t):
            query_copy(pair, step).wait_send()
    for copy in [out_copy, query_grad_copy] + last_copies:
        copy.wait()


def hand_over(*refs):
    count = (len(refs) - 2) // 3
    sources, results, held = refs[:count], refs[count : 2 * count], refs[2 * count : 3 * count]
    in_sem, out_sem = refs[3 * count :]
    into = [pltpu.make_async_copy(sources[i], held[i], in_sem.at[i]) for i in range(count)]
    out = [pltpu.make_async_copy(held[i], results[i], out_sem.at[i]) for i in range(count)]
    for copy in into:
        copy.start()
    for i in range(count):
        into[i].wait()
        out[i].start()
    for copy in out:
        copy.wait()


def local(sizes, *arrays):
    n_s, n_f, n_t = sizes
    queries, key_rows = arrays[0], arrays[1]
    rows, width = queries.shape[1], queries.shape[2]
    pairs = width // (PAIR * HEAD_DIM)
    seq = n_f * rows
    low, full = jnp.bfloat16, jnp.float32
    dma = pltpu.SemaphoreType.DMA
    anywhere = pl.BlockSpec(memory_space=pl.ANY)
    elements = rows * (width // HEAD_DIM) * seq
    results = pl.pallas_call(
        functools.partial(kernel, n_s, n_f, n_t),
        out_shape=[
            jax.ShapeDtypeStruct(queries.shape, low),
            jax.ShapeDtypeStruct(queries.shape, low),
            jax.ShapeDtypeStruct(key_rows.shape, low),
            jax.ShapeDtypeStruct(key_rows.shape, low),
        ],
        in_specs=[anywhere] * 9,
        out_specs=[anywhere] * 4,
        scratch_shapes=[
            pltpu.VMEM((rows, width), low),
            pltpu.VMEM((rows, width), low),
            pltpu.VMEM((n_f, 2, rows, HEAD_DIM), low),
            pltpu.VMEM((n_f, 1, rows), jnp.int32),
            pltpu.VMEM((pairs, rows, PAIR * HEAD_DIM), low),
            pltpu.VMEM((n_f, 2, rows, HEAD_DIM), low),
            pltpu.VMEM((n_f, 1, rows), jnp.int32),
            pltpu.VMEM((seq, rows), full),
            pltpu.VMEM((seq, rows), full),
            pltpu.VMEM((HEAD_DIM, seq), low),
            pltpu.VMEM((HEAD_DIM, seq), low),
            pltpu.VMEM((seq, PAIR * rows), full),
            pltpu.VMEM((seq, PAIR * rows), full),
            pltpu.VMEM((seq, pairs * PAIR * rows), low),
            pltpu.VMEM((seq, pairs * PAIR * rows), low),
            pltpu.VMEM((pairs * PAIR * rows, HEAD_DIM), low),
            pltpu.VMEM((pairs * PAIR * rows, HEAD_DIM), low),
            pltpu.VMEM((n_f - 1, 2, rows, HEAD_DIM), low),
            pltpu.VMEM((n_f - 1, 2, rows, HEAD_DIM), low),
            pltpu.VMEM((rows, width), low),
            pltpu.VMEM((rows, width), low),
            pltpu.VMEM((rows, HEAD_DIM), low),
            pltpu.VMEM((rows, HEAD_DIM), low),
            dma((5,)),
            dma((3 * (n_f - 1),)),
            dma((3 * (n_f - 1),)),
            dma((2 * n_t + 1,)),
            dma((2 * n_t + 1,)),
            dma((2 * (n_f - 1),)),
            dma((2 * (n_f - 1),)),
            dma((pairs, n_t)),
            dma((pairs, n_t)),
            dma((n_f - 1,)),
            dma((n_f - 1,)),
        ],
        compiler_params=pltpu.CompilerParams(
            collective_id=0, has_side_effects=True, vmem_limit_bytes=VMEM_BYTES
        ),
        cost_estimate=pl.CostEstimate(
            flops=14 * elements * HEAD_DIM,
            bytes_accessed=6 * rows * width * 2,
            transcendentals=2 * elements,
        ),
        name="tick",
    )(*arrays)
    return pl.pallas_call(
        hand_over,
        out_shape=[jax.ShapeDtypeStruct(result.shape, low) for result in results],
        in_specs=[anywhere] * len(results),
        out_specs=[anywhere] * len(results),
        scratch_shapes=[pltpu.VMEM(result.shape, low) for result in results]
        + [dma((len(results),)), dma((len(results),))],
        compiler_params=pltpu.CompilerParams(vmem_limit_bytes=VMEM_BYTES),
        name="hand_over",
    )(*results)


def solution(mesh):
    sizes = (mesh.shape["section"], mesh.shape["fsdp"], mesh.shape["tp"])
    by_head = P("section", "fsdp", "tp")
    by_row = P("section", ("fsdp", "tp"), None)
    ids = P("section", "fsdp")
    return jax.shard_map(
        functools.partial(local, sizes),
        mesh=mesh,
        in_specs=(by_head, by_head, by_head, ids, by_row, by_row, by_row, ids, by_head),
        out_specs=(by_head,) * 4,
        check_vma=False,
    )
```

```python
import functools
import math

import jax
import jax.numpy as jnp
from jax import lax
from jax.experimental import pallas as pl
from jax.experimental.pallas import tpu as pltpu
from jax.sharding import PartitionSpec as P

HEAD_DIM = 128
PAIR = 2
WIDE = 4
NEG = -1e30
SCALE = 1.0 / math.sqrt(HEAD_DIM)
SCALE_LOG2 = SCALE * math.log2(math.e)
MESH = pl.DeviceIdType.MESH
VMEM_BYTES = 63 * 1024 * 1024

NT = (((1,), (1,)), ((), ()))


def dot(left, right, dims=(((1,), (0,)), ((), ()))):
    return lax.dot_general(left, right, dims, preferred_element_type=jnp.float32)


def kernel(
    n_s,
    n_f,
    n_t,
    q_ref,
    k_ref,
    v_ref,
    sg_ref,
    hq_ref,
    hk_ref,
    hv_ref,
    hs_ref,
    do_ref,
    o_ref,
    dq_ref,
    dk_ref,
    dv_ref,
    q_buf,
    g_buf,
    kv_fwd,
    sg_fwd,
    hq_buf,
    kv_held,
    sg_held,
    bias,
    bias_held,
    turned,
    turned_held,
    s_buf,
    p_buf,
    p_low,
    d_low,
    q_stack,
    g_stack,
    part_out,
    part_in,
    sums,
    local_sem,
    fwd_send,
    fwd_recv,
    one_send,
    one_recv,
    two_send,
    two_recv,
    hq_send,
    hq_recv,
    red_send,
    red_recv,
):
    rows = q_ref.shape[1]
    part_rows = hq_ref.shape[1]
    width = q_ref.shape[2]
    pair_width = PAIR * HEAD_DIM
    pairs = width // pair_width
    seq = n_f * rows
    block = min(512, seq)
    blocks = seq // block

    s, f, t = lax.axis_index("section"), lax.axis_index("fsdp"), lax.axis_index("tp")
    mirror = n_s - 1 - s

    def at_f(step):
        return lax.rem(f + step, n_f)

    def at_t(step):
        return lax.rem(t + step, n_t)

    for b in range(n_f):

        @pl.when(f < b)
        def _(b=b):
            for kv, ids in ((kv_fwd, sg_fwd), (kv_held, sg_held)):
                kv[b] = jnp.zeros_like(kv[b])
                ids[b] = jnp.zeros_like(ids[b])

    local = [
        pltpu.make_async_copy(k_ref.at[0], kv_fwd.at[f, 0], local_sem.at[0]),
        pltpu.make_async_copy(v_ref.at[0], kv_fwd.at[f, 1], local_sem.at[1]),
        pltpu.make_async_copy(sg_ref, sg_fwd.at[f], local_sem.at[2]),
        pltpu.make_async_copy(q_ref.at[0], q_buf, local_sem.at[3]),
        pltpu.make_async_copy(do_ref.at[0], g_buf, local_sem.at[4]),
    ]
    for copy in local:
        copy.start()

    barrier = pltpu.get_barrier_semaphore()
    for step in range(n_t):
        pl.semaphore_signal(
            barrier, inc=1, device_id=(mirror, f, at_t(step)), device_id_type=MESH
        )
    for step in range(1, n_f):
        pl.semaphore_signal(barrier, inc=1, device_id=(s, at_f(step), t), device_id_type=MESH)
    pl.semaphore_wait(barrier, n_t + n_f - 1)

    def remote(src, dst, send_sem, recv_sem, device):
        return pltpu.make_async_remote_copy(
            src_ref=src,
            dst_ref=dst,
            send_sem=send_sem,
            recv_sem=recv_sem,
            device_id=device,
            device_id_type=MESH,
        )

    own_rows = pl.ds(pl.multiple_of(t * part_rows, part_rows), part_rows)

    first = []
    for step in range(n_t):
        to = at_t(step)
        columns = pl.ds(pl.multiple_of(to * HEAD_DIM, HEAD_DIM), HEAD_DIM)
        for which, held in enumerate((hk_ref, hv_ref)):
            first.append(
                remote(
                    held.at[0, :, columns],
                    kv_held.at[f, which, own_rows, :],
                    one_send.at[2 * step + which],
                    one_recv.at[2 * step + which],
                    (mirror, f, to),
                )
            )
    first.append(
        remote(
            hs_ref,
            sg_held.at[f],
            one_send.at[2 * n_t],
            one_recv.at[2 * n_t],
            (mirror, f, t),
        )
    )
    for copy in first:
        copy.start()

    def fwd_copies(step):
        return [
            remote(
                src,
                sg_fwd.at[f] if which == 2 else kv_fwd.at[f, which],
                fwd_send.at[step - 1, which],
                fwd_recv.at[step - 1, which],
                (s, at_f(step), t),
            )
            for which, src in enumerate((k_ref.at[0], v_ref.at[0], sg_ref))
        ]

    def send_later(copies_of):
        for step in range(n_f - 1, 0, -1):

            @pl.when(f + step < n_f)
            def _(step=step):
                for copy in copies_of(step):
                    copy.start()

    def take_earlier(copies_of):
        for step in range(1, n_f):

            @pl.when(f - step >= 0)
            def _(step=step):
                for copy in copies_of(step):
                    copy.wait_recv()

    send_later(fwd_copies)

    def query_copy(pair, step):
        to = at_t(step)
        columns = pl.ds(
            pl.multiple_of(to * width + pair * pair_width, pair_width), pair_width
        )
        return remote(
            hq_ref.at[0, :, columns],
            hq_buf.at[pair, own_rows, :],
            hq_send.at[pair, step],
            hq_recv.at[pair, step],
            (mirror, f, to),
        )

    for pair in range(pairs):
        for step in range(n_t):
            query_copy(pair, step).start()

    for copy in first:
        copy.wait_recv()
    def held_copies(step):
        return [
            remote(
                buffer.at[f],
                buffer.at[f],
                two_send.at[step - 1, which],
                two_recv.at[step - 1, which],
                (s, at_f(step), t),
            )
            for which, buffer in enumerate((kv_held, sg_held))
        ]

    send_later(held_copies)

    def make_bias(ids, bias):
        own = ids[f]
        for b in range(n_f):
            key_ids = jnp.transpose(jnp.broadcast_to(ids[b], (rows, rows)))
            key_pos = b * rows + lax.broadcasted_iota(jnp.int32, (rows, rows), 0)
            own_pos = f * rows + lax.broadcasted_iota(jnp.int32, (rows, rows), 1)
            seen = (key_pos <= own_pos) & (key_ids == own)
            bias[b * rows : (b + 1) * rows, :] = jnp.where(seen, 0.0, NEG)

    def over_blocks(step, start):
        if blocks == 1:
            return step(0, start)
        return lax.fori_loop(0, blocks, step, start)

    def span(b):
        if blocks == 1:
            return pl.ds(0, block)
        return pl.ds(pl.multiple_of(b * block, block), block)

    def piece(kv, which, b):
        per = block // rows
        if blocks == 1:
            part = kv[:, which]
        else:
            part = kv[pl.ds(b * per, per), which]
        return part.reshape(block, HEAD_DIM)

    def turn(kv, which, turned):
        for b in range(n_f):
            turned[:, b * rows : (b + 1) * rows] = jnp.transpose(kv[b, which])

    def stacked(pair_block):
        return jnp.concatenate(
            [
                pair_block[:, h * HEAD_DIM : (h + 1) * HEAD_DIM]
                for h in range(pair_block.shape[1] // HEAD_DIM)
            ],
            axis=0,
        )

    def scores_of(kv, query, bias):
        def step(b, top):
            masked = jnp.concatenate([bias[span(b), :]] * (query.shape[0] // rows), axis=1)
            scores = dot(piece(kv, 0, b), query, NT) * SCALE_LOG2 + masked
            s_buf[span(b), : query.shape[0]] = scores
            return jnp.maximum(top, jnp.max(scores, axis=0, keepdims=True))

        return over_blocks(step, jnp.full((1, query.shape[0]), NEG, jnp.float32))

    def untangled(wide):
        return jnp.concatenate(
            [
                jnp.transpose(wide[:, h * rows : (h + 1) * rows])
                for h in range(wide.shape[1] // rows)
            ],
            axis=1,
        ).astype(jnp.bfloat16)

    def lanes_of(pair):
        return pl.ds(pl.multiple_of(pair * pair_width, pair_width), pair_width)

    for copy in local:
        copy.wait()
    take_earlier(fwd_copies)
    make_bias(sg_fwd, bias)
    turn(kv_fwd, 1, turned)

    def wide_lanes(index):
        return pl.ds(pl.multiple_of(index * WIDE * HEAD_DIM, WIDE * HEAD_DIM), WIDE * HEAD_DIM)

    def forward_pair(index, carry):
        query = stacked(q_buf[:, wide_lanes(index)])
        top = scores_of(kv_fwd, query, bias)

        def step(b, sums):
            total, out = sums
            weights = jnp.exp2(s_buf[span(b), : WIDE * rows] - top)
            total = total + jnp.sum(weights, axis=0, keepdims=True)
            out = out + dot(turned[:, span(b)], weights.astype(jnp.bfloat16))
            return total, out

        total, out = over_blocks(
            step,
            (
                jnp.zeros((1, WIDE * rows), jnp.float32),
                jnp.zeros((HEAD_DIM, WIDE * rows), jnp.float32),
            ),
        )
        o_ref[0, :, wide_lanes(index)] = untangled(out * (1.0 / total))
        return carry

    wides = width // (WIDE * HEAD_DIM)
    lax.fori_loop(0, wides // 2, forward_pair, 0)

    take_earlier(held_copies)
    make_bias(sg_held, bias_held)

    def columns_of(pair):
        return pl.ds(pl.multiple_of(pair * (PAIR * rows), PAIR * rows), PAIR * rows)

    def backward_pair(pair, carry):
        grad = stacked(g_buf[:, lanes_of(pair)])
        g_stack[columns_of(pair), :] = grad
        for step in range(n_t):
            query_copy(pair, step).wait_recv()
        query = stacked(hq_buf[pair])
        q_stack[columns_of(pair), :] = query
        top = scores_of(kv_held, query, bias_held)

        def middle(b, sums):
            total, along = sums
            weights = jnp.exp2(s_buf[span(b), : PAIR * rows] - top)
            prob_grad = dot(piece(kv_held, 1, b), grad, NT)
            s_buf[span(b), : PAIR * rows] = weights
            p_buf[span(b), :] = prob_grad
            total = total + jnp.sum(weights, axis=0, keepdims=True)
            along = along + jnp.sum(weights * prob_grad, axis=0, keepdims=True)
            return total, along

        zero = jnp.zeros((1, PAIR * rows), jnp.float32)
        total, along = over_blocks(middle, (zero, zero))
        inverse = 1.0 / total
        delta = along * inverse

        def last(b, carry):
            probs = s_buf[span(b), : PAIR * rows] * inverse
            score_grad = probs * (p_buf[span(b), :] - delta)
            p_low[span(b), columns_of(pair)] = probs.astype(jnp.bfloat16)
            d_low[span(b), columns_of(pair)] = score_grad.astype(jnp.bfloat16)
            return carry

        over_blocks(last, 0)
        return carry

    lax.fori_loop(0, pairs, backward_pair, 0)

    def rows_at(index):
        return pl.ds(pl.multiple_of(index * rows, rows), rows)

    def terms(index):
        key_part = dot(d_low[rows_at(index), :], q_stack[...])
        value_part = dot(p_low[rows_at(index), :], g_stack[...])
        return key_part, value_part

    def reduce_copy(step):
        return remote(
            part_out.at[step - 1],
            part_in.at[step - 1],
            red_send.at[step - 1],
            red_recv.at[step - 1],
            (s, lax.rem(f + n_f - step, n_f), t),
        )

    for step in range(n_f - 1, 0, -1):

        @pl.when(f - step >= 0)
        def _(step=step):
            key_part, value_part = terms(lax.rem(f + n_f - step, n_f))
            part_out[step - 1, 0] = key_part.astype(jnp.bfloat16)
            part_out[step - 1, 1] = value_part.astype(jnp.bfloat16)
            reduce_copy(step).start()

    turn(kv_held, 0, turned_held)

    def query_pair(pair, carry):
        def step(b, query_sum):
            return query_sum + dot(turned_held[:, span(b)], d_low[span(b), columns_of(pair)])

        query_sum = over_blocks(step, jnp.zeros((HEAD_DIM, PAIR * rows), jnp.float32))
        dq_ref[0, :, lanes_of(pair)] = untangled(query_sum * SCALE)
        return carry

    lax.fori_loop(0, pairs, query_pair, 0)
    lax.fori_loop(wides // 2, wides, forward_pair, 0)

    key_sum, value_sum = terms(f)
    sums[0] = key_sum
    sums[1] = value_sum
    for step in range(1, n_f):

        @pl.when(f + step < n_f)
        def _(step=step):
            reduce_copy(step).wait_recv()
            sums[...] += part_in[step - 1].astype(jnp.float32)

    dk_ref[0] = (sums[0] * SCALE).astype(jnp.bfloat16)
    dv_ref[0] = sums[1].astype(jnp.bfloat16)
    for copy in first:
        copy.wait_send()
    for step in range(1, n_f):

        @pl.when(f + step < n_f)
        def _(step=step):
            for copy in fwd_copies(step) + held_copies(step):
                copy.wait_send()

        @pl.when(f - step >= 0)
        def _(step=step):
            reduce_copy(step).wait_send()

    for pair in range(pairs):
        for step in range(n_t):
            query_copy(pair, step).wait_send()


def hand_over(*refs):
    count = len(refs) // 2
    sems = refs[-1]
    copies = [
        pltpu.make_async_copy(refs[i], refs[count + i], sems.at[i]) for i in range(count)
    ]
    for copy in copies:
        copy.start()
    for copy in copies:
        copy.wait()


def local(sizes, *arrays):
    n_s, n_f, n_t = sizes
    queries, key_rows = arrays[0], arrays[1]
    rows, width = queries.shape[1], queries.shape[2]
    pairs = width // (PAIR * HEAD_DIM)
    seq = n_f * rows
    low, full = jnp.bfloat16, jnp.float32
    dma = pltpu.SemaphoreType.DMA
    anywhere = pl.BlockSpec(memory_space=pl.ANY)
    inside = pl.BlockSpec(memory_space=pltpu.VMEM)
    elements = rows * (width // HEAD_DIM) * seq
    results = pl.pallas_call(
        functools.partial(kernel, n_s, n_f, n_t),
        out_shape=[
            pltpu.VMEM(queries.shape, low),
            pltpu.VMEM(queries.shape, low),
            pltpu.VMEM(key_rows.shape, low),
            pltpu.VMEM(key_rows.shape, low),
        ],
        in_specs=[anywhere] * 9,
        out_specs=[inside] * 4,
        scratch_shapes=[
            pltpu.VMEM((rows, width), low),
            pltpu.VMEM((rows, width), low),
            pltpu.VMEM((n_f, 2, rows, HEAD_DIM), low),
            pltpu.VMEM((n_f, 1, rows), jnp.int32),
            pltpu.VMEM((pairs, rows, PAIR * HEAD_DIM), low),
            pltpu.VMEM((n_f, 2, rows, HEAD_DIM), low),
            pltpu.VMEM((n_f, 1, rows), jnp.int32),
            pltpu.VMEM((seq, rows), full),
            pltpu.VMEM((seq, rows), full),
            pltpu.VMEM((HEAD_DIM, seq), low),
            pltpu.VMEM((HEAD_DIM, seq), low),
            pltpu.VMEM((seq, WIDE * rows), full),
            pltpu.VMEM((seq, PAIR * rows), full),
            pltpu.VMEM((seq, pairs * PAIR * rows), low),
            pltpu.VMEM((seq, pairs * PAIR * rows), low),
            pltpu.VMEM((pairs * PAIR * rows, HEAD_DIM), low),
            pltpu.VMEM((pairs * PAIR * rows, HEAD_DIM), low),
            pltpu.VMEM((n_f - 1, 2, rows, HEAD_DIM), low),
            pltpu.VMEM((n_f - 1, 2, rows, HEAD_DIM), low),
            pltpu.VMEM((2, rows, HEAD_DIM), full),
            dma((5,)),
            dma((n_f - 1, 3)),
            dma((n_f - 1, 3)),
            dma((2 * n_t + 1,)),
            dma((2 * n_t + 1,)),
            dma((n_f - 1, 2)),
            dma((n_f - 1, 2)),
            dma((pairs, n_t)),
            dma((pairs, n_t)),
            dma((n_f - 1,)),
            dma((n_f - 1,)),
        ],
        compiler_params=pltpu.CompilerParams(
            collective_id=0, has_side_effects=True, vmem_limit_bytes=VMEM_BYTES
        ),
        cost_estimate=pl.CostEstimate(
            flops=14 * elements * HEAD_DIM,
            bytes_accessed=6 * rows * width * 2,
            transcendentals=2 * elements,
        ),
        name="tick",
    )(*arrays)
    return pl.pallas_call(
        hand_over,
        out_shape=[pltpu.HBM(result.shape, low) for result in results],
        in_specs=[inside] * len(results),
        out_specs=[anywhere] * len(results),
        scratch_shapes=[dma((len(results),))],
        compiler_params=pltpu.CompilerParams(vmem_limit_bytes=VMEM_BYTES // 4),
        name="hand_over",
    )(*results)


def solution(mesh):
    sizes = (mesh.shape["section"], mesh.shape["fsdp"], mesh.shape["tp"])
    by_head = P("section", "fsdp", "tp")
    by_row = P("section", ("fsdp", "tp"), None)
    ids = P("section", "fsdp")
    return jax.shard_map(
        functools.partial(local, sizes),
        mesh=mesh,
        in_specs=(by_head, by_head, by_head, ids, by_row, by_row, by_row, ids, by_head),
        out_specs=(by_head,) * 4,
        check_vma=False,
    )
```

```python
import functools
import math

import jax
import jax.numpy as jnp
from jax import lax
from jax.experimental import pallas as pl
from jax.experimental.pallas import tpu as pltpu
from jax.sharding import PartitionSpec as P

HEAD_DIM = 128
PAIR = 2
LOW = 2
WIDE = 4
NEG = -1e30
SCALE = 1.0 / math.sqrt(HEAD_DIM)
SCALE_LOG2 = SCALE * math.log2(math.e)
MESH = pl.DeviceIdType.MESH
VMEM_BYTES = 63 * 1024 * 1024

NT = (((1,), (1,)), ((), ()))


def dot(left, right, dims=(((1,), (0,)), ((), ()))):
    return lax.dot_general(left, right, dims, preferred_element_type=jnp.float32)


def kernel(
    n_s,
    n_f,
    n_t,
    q_ref,
    k_ref,
    v_ref,
    sg_ref,
    hq_ref,
    hk_ref,
    hv_ref,
    hs_ref,
    do_ref,
    o_ref,
    dq_ref,
    dk_ref,
    dv_ref,
    q_buf,
    g_buf,
    kv_fwd,
    sg_fwd,
    hq_buf,
    kv_held,
    sg_held,
    bias,
    bias_held,
    turned,
    turned_held,
    s_buf,
    p_buf,
    p_low,
    d_low,
    q_stack,
    g_stack,
    part_out,
    part_in,
    sums,
    local_sem,
    fwd_send,
    fwd_recv,
    one_send,
    one_recv,
    ids_send,
    ids_recv,
    on_send,
    on_recv,
    two_send,
    two_recv,
    hq_send,
    hq_recv,
    red_send,
    red_recv,
):
    rows = q_ref.shape[1]
    part_rows = hq_ref.shape[1]
    width = q_ref.shape[2]
    pair_width = PAIR * HEAD_DIM
    pairs = width // pair_width
    seq = n_f * rows
    block = min(512, seq)
    blocks = seq // block

    s, f, t = lax.axis_index("section"), lax.axis_index("fsdp"), lax.axis_index("tp")
    mirror = n_s - 1 - s

    def at_f(step):
        return lax.rem(f + step, n_f)

    high = f // LOW
    lane = f - high * LOW
    n_high = n_f // LOW
    sibling = high * LOW + (LOW - 1 - lane)

    def at_t(step):
        return lax.rem(t + step, n_t)

    for b in range(n_f):

        @pl.when(f < b)
        def _(b=b):
            for kv, ids in ((kv_fwd, sg_fwd), (kv_held, sg_held)):
                kv[b] = jnp.zeros_like(kv[b])
                ids[b] = jnp.zeros_like(ids[b])

    local = [
        pltpu.make_async_copy(k_ref.at[0], kv_fwd.at[f, 0], local_sem.at[0]),
        pltpu.make_async_copy(v_ref.at[0], kv_fwd.at[f, 1], local_sem.at[1]),
        pltpu.make_async_copy(sg_ref, sg_fwd.at[f], local_sem.at[2]),
        pltpu.make_async_copy(q_ref.at[0], q_buf, local_sem.at[3]),
        pltpu.make_async_copy(do_ref.at[0], g_buf, local_sem.at[4]),
    ]
    for copy in local:
        copy.start()

    barrier = pltpu.get_barrier_semaphore()
    for step in range(n_t):
        pl.semaphore_signal(
            barrier, inc=1, device_id=(mirror, f, at_t(step)), device_id_type=MESH
        )
    for step in range(1, n_f):
        pl.semaphore_signal(barrier, inc=1, device_id=(s, at_f(step), t), device_id_type=MESH)
    pl.semaphore_wait(barrier, n_t + n_f - 1)

    def remote(src, dst, send_sem, recv_sem, device):
        return pltpu.make_async_remote_copy(
            src_ref=src,
            dst_ref=dst,
            send_sem=send_sem,
            recv_sem=recv_sem,
            device_id=device,
            device_id_type=MESH,
        )

    own_rows = pl.ds(pl.multiple_of(t * part_rows, part_rows), part_rows)

    first = []
    for step in range(n_t):
        to = at_t(step)
        columns = pl.ds(pl.multiple_of(to * HEAD_DIM, HEAD_DIM), HEAD_DIM)
        for which, held in enumerate((hk_ref, hv_ref)):
            first.append(
                remote(
                    held.at[0, :, columns],
                    kv_held.at[f, which, own_rows, :],
                    one_send.at[2 * step + which],
                    one_recv.at[2 * step + which],
                    (mirror, f, to),
                )
            )
    first.append(
        remote(
            hs_ref,
            sg_held.at[f],
            one_send.at[2 * n_t],
            one_recv.at[2 * n_t],
            (mirror, f, t),
        )
    )
    for copy in first:
        copy.start()

    def fwd_copies(at, device):
        return [
            remote(
                src.at[0],
                kv_fwd.at[f, which],
                fwd_send.at[at, which],
                fwd_recv.at[at, which],
                (s, device, t),
            )
            for which, src in enumerate((k_ref, v_ref))
        ]

    def across(step):
        return fwd_copies(step, lax.rem(high + step, n_high) * LOW + lane)

    def passed_on(step):
        block_at = lax.rem(high + n_high - step, n_high) * LOW + lane
        return remote(
            kv_fwd.at[block_at],
            kv_fwd.at[block_at],
            on_send.at[step - 1],
            on_recv.at[step - 1],
            (s, sibling, t),
        )

    def fwd_ids(step):
        return [
            remote(
                sg_ref,
                sg_fwd.at[f],
                ids_send.at[step - 1],
                ids_recv.at[step - 1],
                (s, at_f(step), t),
            )
        ]

    def send_later(copies_of):
        for step in range(n_f - 1, 0, -1):

            @pl.when(f + step < n_f)
            def _(step=step):
                for copy in copies_of(step):
                    copy.start()

    def take_earlier(copies_of):
        for step in range(1, n_f):

            @pl.when(f - step >= 0)
            def _(step=step):
                for copy in copies_of(step):
                    copy.wait_recv()

    for step in range(n_high - 1, 0, -1):

        @pl.when(high + step < n_high)
        def _(step=step):
            for copy in across(step):
                copy.start()

    @pl.when(lane == 0)
    def _():
        for copy in fwd_copies(0, sibling):
            copy.start()

    send_later(fwd_ids)

    def query_copy(pair, step):
        to = at_t(step)
        columns = pl.ds(
            pl.multiple_of(to * width + pair * pair_width, pair_width), pair_width
        )
        return remote(
            hq_ref.at[0, :, columns],
            hq_buf.at[pair, own_rows, :],
            hq_send.at[pair, step],
            hq_recv.at[pair, step],
            (mirror, f, to),
        )

    for copy in first:
        copy.wait_recv()
    def held_copies(step):
        return [
            remote(
                buffer.at[f],
                buffer.at[f],
                two_send.at[step - 1, which],
                two_recv.at[step - 1, which],
                (s, at_f(step), t),
            )
            for which, buffer in enumerate((kv_held, sg_held))
        ]

    send_later(held_copies)

    for pair in range(pairs):
        for step in range(n_t):
            query_copy(pair, step).start()

    for step in range(1, n_high):

        @pl.when(high - step >= 0)
        def _(step=step):
            for copy in across(step):
                copy.wait_recv()
            passed_on(step).start()


    def make_bias(ids, bias):
        own = ids[f]
        for b in range(n_f):
            key_ids = jnp.transpose(jnp.broadcast_to(ids[b], (rows, rows)))
            key_pos = b * rows + lax.broadcasted_iota(jnp.int32, (rows, rows), 0)
            own_pos = f * rows + lax.broadcasted_iota(jnp.int32, (rows, rows), 1)
            seen = (key_pos <= own_pos) & (key_ids == own)
            bias[b * rows : (b + 1) * rows, :] = jnp.where(seen, 0.0, NEG)

    def over_blocks(step, start):
        if blocks == 1:
            return step(0, start)
        return lax.fori_loop(0, blocks, step, start)

    def span(b):
        if blocks == 1:
            return pl.ds(0, block)
        return pl.ds(pl.multiple_of(b * block, block), block)

    def piece(kv, which, b):
        per = block // rows
        if blocks == 1:
            part = kv[:, which]
        else:
            part = kv[pl.ds(b * per, per), which]
        return part.reshape(block, HEAD_DIM)

    def turn(kv, which, turned):
        for b in range(n_f):
            turned[:, b * rows : (b + 1) * rows] = jnp.transpose(kv[b, which])

    def stacked(pair_block):
        return jnp.concatenate(
            [
                pair_block[:, h * HEAD_DIM : (h + 1) * HEAD_DIM]
                for h in range(pair_block.shape[1] // HEAD_DIM)
            ],
            axis=0,
        )

    def scores_of(kv, query, bias):
        def step(b, top):
            masked = jnp.concatenate([bias[span(b), :]] * (query.shape[0] // rows), axis=1)
            scores = dot(piece(kv, 0, b), query, NT) * SCALE_LOG2 + masked
            s_buf[span(b), : query.shape[0]] = scores
            return jnp.maximum(top, jnp.max(scores, axis=0, keepdims=True))

        return over_blocks(step, jnp.full((1, query.shape[0]), NEG, jnp.float32))

    def untangled(wide):
        return jnp.concatenate(
            [
                jnp.transpose(wide[:, h * rows : (h + 1) * rows])
                for h in range(wide.shape[1] // rows)
            ],
            axis=1,
        ).astype(jnp.bfloat16)

    def lanes_of(pair):
        return pl.ds(pl.multiple_of(pair * pair_width, pair_width), pair_width)

    for copy in local:
        copy.wait()
    take_earlier(fwd_ids)
    make_bias(sg_fwd, bias)

    @pl.when(lane == LOW - 1)
    def _():
        for copy in fwd_copies(0, sibling):
            copy.wait_recv()

    for step in range(1, n_high):

        @pl.when(high - step >= 0)
        def _(step=step):
            passed_on(step).wait_recv()

    turn(kv_fwd, 1, turned)

    def wide_lanes(index):
        return pl.ds(pl.multiple_of(index * WIDE * HEAD_DIM, WIDE * HEAD_DIM), WIDE * HEAD_DIM)

    def forward_pair(index, carry):
        query = stacked(q_buf[:, wide_lanes(index)])
        top = scores_of(kv_fwd, query, bias)

        def step(b, sums):
            total, out = sums
            weights = jnp.exp2(s_buf[span(b), : WIDE * rows] - top)
            total = total + jnp.sum(weights, axis=0, keepdims=True)
            out = out + dot(turned[:, span(b)], weights.astype(jnp.bfloat16))
            return total, out

        total, out = over_blocks(
            step,
            (
                jnp.zeros((1, WIDE * rows), jnp.float32),
                jnp.zeros((HEAD_DIM, WIDE * rows), jnp.float32),
            ),
        )
        o_ref[0, :, wide_lanes(index)] = untangled(out * (1.0 / total))
        return carry

    wides = width // (WIDE * HEAD_DIM)
    lax.fori_loop(0, wides // 2, forward_pair, 0)

    take_earlier(held_copies)
    make_bias(sg_held, bias_held)

    def columns_of(pair):
        return pl.ds(pl.multiple_of(pair * (PAIR * rows), PAIR * rows), PAIR * rows)

    def backward_pair(pair, carry):
        grad = stacked(g_buf[:, lanes_of(pair)])
        g_stack[columns_of(pair), :] = grad
        for step in range(n_t):
            query_copy(pair, step).wait_recv()
        query = stacked(hq_buf[pair])
        q_stack[columns_of(pair), :] = query
        top = scores_of(kv_held, query, bias_held)

        def middle(b, sums):
            total, along = sums
            weights = jnp.exp2(s_buf[span(b), : PAIR * rows] - top)
            prob_grad = dot(piece(kv_held, 1, b), grad, NT)
            s_buf[span(b), : PAIR * rows] = weights
            p_buf[span(b), :] = prob_grad
            total = total + jnp.sum(weights, axis=0, keepdims=True)
            along = along + jnp.sum(weights * prob_grad, axis=0, keepdims=True)
            return total, along

        zero = jnp.zeros((1, PAIR * rows), jnp.float32)
        total, along = over_blocks(middle, (zero, zero))
        inverse = 1.0 / total
        delta = along * inverse

        def last(b, carry):
            probs = s_buf[span(b), : PAIR * rows] * inverse
            score_grad = probs * (p_buf[span(b), :] - delta)
            p_low[span(b), columns_of(pair)] = probs.astype(jnp.bfloat16)
            d_low[span(b), columns_of(pair)] = score_grad.astype(jnp.bfloat16)
            return carry

        over_blocks(last, 0)
        return carry

    lax.fori_loop(0, pairs, backward_pair, 0)

    def rows_at(index):
        return pl.ds(pl.multiple_of(index * rows, rows), rows)

    def terms(index):
        key_part = dot(d_low[rows_at(index), :], q_stack[...])
        value_part = dot(p_low[rows_at(index), :], g_stack[...])
        return key_part, value_part

    def reduce_copy(step):
        return remote(
            part_out.at[step - 1],
            part_in.at[step - 1],
            red_send.at[step - 1],
            red_recv.at[step - 1],
            (s, lax.rem(f + n_f - step, n_f), t),
        )

    for step in range(n_f - 1, 0, -1):

        @pl.when(f - step >= 0)
        def _(step=step):
            key_part, value_part = terms(lax.rem(f + n_f - step, n_f))
            part_out[step - 1, 0] = key_part.astype(jnp.bfloat16)
            part_out[step - 1, 1] = value_part.astype(jnp.bfloat16)
            reduce_copy(step).start()

    turn(kv_held, 0, turned_held)

    def query_pair(pair, carry):
        def step(b, query_sum):
            return query_sum + dot(turned_held[:, span(b)], d_low[span(b), columns_of(pair)])

        query_sum = over_blocks(step, jnp.zeros((HEAD_DIM, PAIR * rows), jnp.float32))
        dq_ref[0, :, lanes_of(pair)] = untangled(query_sum * SCALE)
        return carry

    lax.fori_loop(0, pairs, query_pair, 0)
    lax.fori_loop(wides // 2, wides, forward_pair, 0)

    key_sum, value_sum = terms(f)
    sums[0] = key_sum
    sums[1] = value_sum
    for step in range(1, n_f):

        @pl.when(f + step < n_f)
        def _(step=step):
            reduce_copy(step).wait_recv()
            sums[...] += part_in[step - 1].astype(jnp.float32)

    dk_ref[0] = (sums[0] * SCALE).astype(jnp.bfloat16)
    dv_ref[0] = sums[1].astype(jnp.bfloat16)
    for copy in first:
        copy.wait_send()

    @pl.when(lane == 0)
    def _():
        for copy in fwd_copies(0, sibling):
            copy.wait_send()

    for step in range(1, n_high):

        @pl.when(high + step < n_high)
        def _(step=step):
            for copy in across(step):
                copy.wait_send()

        @pl.when(high - step >= 0)
        def _(step=step):
            passed_on(step).wait_send()

    for step in range(1, n_f):

        @pl.when(f + step < n_f)
        def _(step=step):
            for copy in fwd_ids(step) + held_copies(step):
                copy.wait_send()

        @pl.when(f - step >= 0)
        def _(step=step):
            reduce_copy(step).wait_send()

    for pair in range(pairs):
        for step in range(n_t):
            query_copy(pair, step).wait_send()


def hand_over(*refs):
    count = len(refs) // 2
    sems = refs[-1]
    copies = [
        pltpu.make_async_copy(refs[i], refs[count + i], sems.at[i]) for i in range(count)
    ]
    for copy in copies:
        copy.start()
    for copy in copies:
        copy.wait()


def local(sizes, *arrays):
    n_s, n_f, n_t = sizes
    queries, key_rows = arrays[0], arrays[1]
    rows, width = queries.shape[1], queries.shape[2]
    pairs = width // (PAIR * HEAD_DIM)
    seq = n_f * rows
    low, full = jnp.bfloat16, jnp.float32
    dma = pltpu.SemaphoreType.DMA
    anywhere = pl.BlockSpec(memory_space=pl.ANY)
    inside = pl.BlockSpec(memory_space=pltpu.VMEM)
    elements = rows * (width // HEAD_DIM) * seq
    results = pl.pallas_call(
        functools.partial(kernel, n_s, n_f, n_t),
        out_shape=[
            pltpu.VMEM(queries.shape, low),
            pltpu.VMEM(queries.shape, low),
            pltpu.VMEM(key_rows.shape, low),
            pltpu.VMEM(key_rows.shape, low),
        ],
        in_specs=[anywhere] * 9,
        out_specs=[inside] * 4,
        scratch_shapes=[
            pltpu.VMEM((rows, width), low),
            pltpu.VMEM((rows, width), low),
            pltpu.VMEM((n_f, 2, rows, HEAD_DIM), low),
            pltpu.VMEM((n_f, 1, rows), jnp.int32),
            pltpu.VMEM((pairs, rows, PAIR * HEAD_DIM), low),
            pltpu.VMEM((n_f, 2, rows, HEAD_DIM), low),
            pltpu.VMEM((n_f, 1, rows), jnp.int32),
            pltpu.VMEM((seq, rows), full),
            pltpu.VMEM((seq, rows), full),
            pltpu.VMEM((HEAD_DIM, seq), low),
            pltpu.VMEM((HEAD_DIM, seq), low),
            pltpu.VMEM((seq, WIDE * rows), full),
            pltpu.VMEM((seq, PAIR * rows), full),
            pltpu.VMEM((seq, pairs * PAIR * rows), low),
            pltpu.VMEM((seq, pairs * PAIR * rows), low),
            pltpu.VMEM((pairs * PAIR * rows, HEAD_DIM), low),
            pltpu.VMEM((pairs * PAIR * rows, HEAD_DIM), low),
            pltpu.VMEM((n_f - 1, 2, rows, HEAD_DIM), low),
            pltpu.VMEM((n_f - 1, 2, rows, HEAD_DIM), low),
            pltpu.VMEM((2, rows, HEAD_DIM), full),
            dma((5,)),
            dma((n_f // LOW, 2)),
            dma((n_f // LOW, 2)),
            dma((2 * n_t + 1,)),
            dma((2 * n_t + 1,)),
            dma((n_f - 1,)),
            dma((n_f - 1,)),
            dma((n_f // LOW - 1,)),
            dma((n_f // LOW - 1,)),
            dma((n_f - 1, 2)),
            dma((n_f - 1, 2)),
            dma((pairs, n_t)),
            dma((pairs, n_t)),
            dma((n_f - 1,)),
            dma((n_f - 1,)),
        ],
        compiler_params=pltpu.CompilerParams(
            collective_id=0, has_side_effects=True, vmem_limit_bytes=VMEM_BYTES
        ),
        cost_estimate=pl.CostEstimate(
            flops=14 * elements * HEAD_DIM,
            bytes_accessed=6 * rows * width * 2,
            transcendentals=2 * elements,
        ),
        name="tick",
    )(*arrays)
    return pl.pallas_call(
        hand_over,
        out_shape=[pltpu.HBM(result.shape, low) for result in results],
        in_specs=[inside] * len(results),
        out_specs=[anywhere] * len(results),
        scratch_shapes=[dma((len(results),))],
        compiler_params=pltpu.CompilerParams(vmem_limit_bytes=VMEM_BYTES // 4),
        name="hand_over",
    )(*results)


def solution(mesh):
    sizes = (mesh.shape["section"], mesh.shape["fsdp"], mesh.shape["tp"])
    by_head = P("section", "fsdp", "tp")
    by_row = P("section", ("fsdp", "tp"), None)
    ids = P("section", "fsdp")
    return jax.shard_map(
        functools.partial(local, sizes),
        mesh=mesh,
        in_specs=(by_head, by_head, by_head, ids, by_row, by_row, by_row, ids, by_head),
        out_specs=(by_head,) * 4,
        check_vma=False,
    )
```

```python
import functools
import math

import jax
import jax.numpy as jnp
from jax import lax
from jax.experimental import pallas as pl
from jax.experimental.pallas import tpu as pltpu
from jax.sharding import PartitionSpec as P

HEAD_DIM = 128
PAIR = 2
LOW = 2
WIDE = 4
NEG = -1e30
SCALE = 1.0 / math.sqrt(HEAD_DIM)
SCALE_LOG2 = SCALE * math.log2(math.e)
MESH = pl.DeviceIdType.MESH
VMEM_BYTES = 63 * 1024 * 1024

NT = (((1,), (1,)), ((), ()))


def dot(left, right, dims=(((1,), (0,)), ((), ()))):
    return lax.dot_general(left, right, dims, preferred_element_type=jnp.float32)


def kernel(
    n_s,
    n_f,
    n_t,
    q_ref,
    k_ref,
    v_ref,
    sg_ref,
    hq_ref,
    hk_ref,
    hv_ref,
    hs_ref,
    do_ref,
    o_ref,
    dq_ref,
    dk_ref,
    dv_ref,
    q_buf,
    g_buf,
    kv_fwd,
    sg_fwd,
    hq_buf,
    kv_held,
    sg_held,
    bias,
    bias_held,
    turned,
    turned_held,
    s_buf,
    p_buf,
    p_low,
    d_low,
    q_stack,
    g_stack,
    part_out,
    part_in,
    sums,
    local_sem,
    fwd_send,
    fwd_recv,
    one_send,
    one_recv,
    ids_send,
    ids_recv,
    on_send,
    on_recv,
    two_send,
    two_recv,
    hq_send,
    hq_recv,
    red_send,
    red_recv,
):
    rows = q_ref.shape[1]
    part_rows = hq_ref.shape[1]
    width = q_ref.shape[2]
    pair_width = PAIR * HEAD_DIM
    pairs = width // pair_width
    seq = n_f * rows
    block = min(512, seq)
    blocks = seq // block

    s, f, t = lax.axis_index("section"), lax.axis_index("fsdp"), lax.axis_index("tp")
    mirror = n_s - 1 - s

    def at_f(step):
        return lax.rem(f + step, n_f)

    high = f // LOW
    lane = f - high * LOW
    n_high = n_f // LOW
    sibling = high * LOW + (LOW - 1 - lane)

    def at_t(step):
        return lax.rem(t + step, n_t)

    for b in range(n_f):

        @pl.when(f < b)
        def _(b=b):
            for kv, ids in ((kv_fwd, sg_fwd), (kv_held, sg_held)):
                kv[b] = jnp.zeros_like(kv[b])
                ids[b] = jnp.zeros_like(ids[b])

    local = [
        pltpu.make_async_copy(k_ref.at[0], kv_fwd.at[f, 0], local_sem.at[0]),
        pltpu.make_async_copy(v_ref.at[0], kv_fwd.at[f, 1], local_sem.at[1]),
        pltpu.make_async_copy(sg_ref, sg_fwd.at[f], local_sem.at[2]),
        pltpu.make_async_copy(q_ref.at[0], q_buf, local_sem.at[3]),
        pltpu.make_async_copy(do_ref.at[0], g_buf, local_sem.at[4]),
    ]
    for copy in local:
        copy.start()

    barrier = pltpu.get_barrier_semaphore()
    for step in range(n_t):
        pl.semaphore_signal(
            barrier, inc=1, device_id=(mirror, f, at_t(step)), device_id_type=MESH
        )
    for step in range(1, n_f):
        pl.semaphore_signal(barrier, inc=1, device_id=(s, at_f(step), t), device_id_type=MESH)
    pl.semaphore_wait(barrier, n_t + n_f - 1)

    def remote(src, dst, send_sem, recv_sem, device):
        return pltpu.make_async_remote_copy(
            src_ref=src,
            dst_ref=dst,
            send_sem=send_sem,
            recv_sem=recv_sem,
            device_id=device,
            device_id_type=MESH,
        )

    own_rows = pl.ds(pl.multiple_of(t * part_rows, part_rows), part_rows)

    first = []
    for step in range(n_t):
        to = at_t(step)
        columns = pl.ds(pl.multiple_of(to * HEAD_DIM, HEAD_DIM), HEAD_DIM)
        for which, held in enumerate((hk_ref, hv_ref)):
            first.append(
                remote(
                    held.at[0, :, columns],
                    kv_held.at[f, which, own_rows, :],
                    one_send.at[2 * step + which],
                    one_recv.at[2 * step + which],
                    (mirror, f, to),
                )
            )
    first.append(
        remote(
            hs_ref,
            sg_held.at[f],
            one_send.at[2 * n_t],
            one_recv.at[2 * n_t],
            (mirror, f, t),
        )
    )
    for copy in first:
        copy.start()

    def query_copy(pair, step):
        to = at_t(step)
        columns = pl.ds(
            pl.multiple_of(to * width + pair * pair_width, pair_width), pair_width
        )
        return remote(
            hq_ref.at[0, :, columns],
            hq_buf.at[pair, own_rows, :],
            hq_send.at[pair, step],
            hq_recv.at[pair, step],
            (mirror, f, to),
        )

    def send_queries(begin, end):
        for pair in range(begin, end):
            for step in range(n_t):
                query_copy(pair, step).start()

    send_queries(0, 1)

    def fwd_copies(at, device):
        return [
            remote(
                src.at[0],
                kv_fwd.at[f, which],
                fwd_send.at[at, which],
                fwd_recv.at[at, which],
                (s, device, t),
            )
            for which, src in enumerate((k_ref, v_ref))
        ]

    def across(step):
        return fwd_copies(step, lax.rem(high + step, n_high) * LOW + lane)

    def passed_on(step):
        block_at = lax.rem(high + n_high - step, n_high) * LOW + lane
        return remote(
            kv_fwd.at[block_at],
            kv_fwd.at[block_at],
            on_send.at[step - 1],
            on_recv.at[step - 1],
            (s, sibling, t),
        )

    def fwd_ids(step):
        return [
            remote(
                sg_ref,
                sg_fwd.at[f],
                ids_send.at[step - 1],
                ids_recv.at[step - 1],
                (s, at_f(step), t),
            )
        ]

    def send_later(copies_of):
        for step in range(n_f - 1, 0, -1):

            @pl.when(f + step < n_f)
            def _(step=step):
                for copy in copies_of(step):
                    copy.start()

    def take_earlier(copies_of):
        for step in range(1, n_f):

            @pl.when(f - step >= 0)
            def _(step=step):
                for copy in copies_of(step):
                    copy.wait_recv()

    for step in range(n_high - 1, 0, -1):

        @pl.when(high + step < n_high)
        def _(step=step):
            for copy in across(step):
                copy.start()


    for copy in first:
        copy.wait_recv()
    def held_copies(step):
        return [
            remote(
                buffer.at[f],
                buffer.at[f],
                two_send.at[step - 1, which],
                two_recv.at[step - 1, which],
                (s, at_f(step), t),
            )
            for which, buffer in enumerate((kv_held, sg_held))
        ]

    send_later(held_copies)

    @pl.when(lane == 0)
    def _():
        for copy in fwd_copies(0, sibling):
            copy.start()

    send_later(fwd_ids)

    send_queries(1, 2)

    for step in range(1, n_high):

        @pl.when(high - step >= 0)
        def _(step=step):
            for copy in across(step):
                copy.wait_recv()
            passed_on(step).start()

    send_queries(2, pairs)


    def make_bias(ids, bias):
        own = ids[f]
        for b in range(n_f):
            key_ids = jnp.transpose(jnp.broadcast_to(ids[b], (rows, rows)))
            key_pos = b * rows + lax.broadcasted_iota(jnp.int32, (rows, rows), 0)
            own_pos = f * rows + lax.broadcasted_iota(jnp.int32, (rows, rows), 1)
            seen = (key_pos <= own_pos) & (key_ids == own)
            bias[b * rows : (b + 1) * rows, :] = jnp.where(seen, 0.0, NEG)

    def over_blocks(step, start):
        if blocks == 1:
            return step(0, start)
        return lax.fori_loop(0, blocks, step, start)

    def span(b):
        if blocks == 1:
            return pl.ds(0, block)
        return pl.ds(pl.multiple_of(b * block, block), block)

    def piece(kv, which, b):
        per = block // rows
        if blocks == 1:
            part = kv[:, which]
        else:
            part = kv[pl.ds(b * per, per), which]
        return part.reshape(block, HEAD_DIM)

    def turn(kv, which, turned):
        for b in range(n_f):
            turned[:, b * rows : (b + 1) * rows] = jnp.transpose(kv[b, which])

    def stacked(pair_block):
        return jnp.concatenate(
            [
                pair_block[:, h * HEAD_DIM : (h + 1) * HEAD_DIM]
                for h in range(pair_block.shape[1] // HEAD_DIM)
            ],
            axis=0,
        )

    def scores_of(kv, query, bias):
        def step(b, top):
            masked = jnp.concatenate([bias[span(b), :]] * (query.shape[0] // rows), axis=1)
            scores = dot(piece(kv, 0, b), query, NT) * SCALE_LOG2 + masked
            s_buf[span(b), : query.shape[0]] = scores
            return jnp.maximum(top, jnp.max(scores, axis=0, keepdims=True))

        return over_blocks(step, jnp.full((1, query.shape[0]), NEG, jnp.float32))

    def untangled(wide):
        return jnp.concatenate(
            [
                jnp.transpose(wide[:, h * rows : (h + 1) * rows])
                for h in range(wide.shape[1] // rows)
            ],
            axis=1,
        ).astype(jnp.bfloat16)

    def lanes_of(pair):
        return pl.ds(pl.multiple_of(pair * pair_width, pair_width), pair_width)

    for copy in local:
        copy.wait()
    take_earlier(fwd_ids)
    make_bias(sg_fwd, bias)

    @pl.when(lane == LOW - 1)
    def _():
        for copy in fwd_copies(0, sibling):
            copy.wait_recv()

    for step in range(1, n_high):

        @pl.when(high - step >= 0)
        def _(step=step):
            passed_on(step).wait_recv()

    turn(kv_fwd, 1, turned)

    def wide_lanes(index):
        return pl.ds(pl.multiple_of(index * WIDE * HEAD_DIM, WIDE * HEAD_DIM), WIDE * HEAD_DIM)

    def forward_pair(index, carry):
        query = stacked(q_buf[:, wide_lanes(index)])
        top = scores_of(kv_fwd, query, bias)

        def step(b, sums):
            total, out = sums
            weights = jnp.exp2(s_buf[span(b), : WIDE * rows] - top)
            total = total + jnp.sum(weights, axis=0, keepdims=True)
            out = out + dot(turned[:, span(b)], weights.astype(jnp.bfloat16))
            return total, out

        total, out = over_blocks(
            step,
            (
                jnp.zeros((1, WIDE * rows), jnp.float32),
                jnp.zeros((HEAD_DIM, WIDE * rows), jnp.float32),
            ),
        )
        o_ref[0, :, wide_lanes(index)] = untangled(out * (1.0 / total))
        return carry

    wides = width // (WIDE * HEAD_DIM)
    lax.fori_loop(0, wides // 2, forward_pair, 0)

    take_earlier(held_copies)
    make_bias(sg_held, bias_held)

    def columns_of(pair):
        return pl.ds(pl.multiple_of(pair * (PAIR * rows), PAIR * rows), PAIR * rows)

    def backward_pair(pair, carry):
        grad = stacked(g_buf[:, lanes_of(pair)])
        g_stack[columns_of(pair), :] = grad
        for step in range(n_t):
            query_copy(pair, step).wait_recv()
        query = stacked(hq_buf[pair])
        q_stack[columns_of(pair), :] = query
        top = scores_of(kv_held, query, bias_held)

        def middle(b, sums):
            total, along = sums
            weights = jnp.exp2(s_buf[span(b), : PAIR * rows] - top)
            prob_grad = dot(piece(kv_held, 1, b), grad, NT)
            s_buf[span(b), : PAIR * rows] = weights
            p_buf[span(b), :] = prob_grad
            total = total + jnp.sum(weights, axis=0, keepdims=True)
            along = along + jnp.sum(weights * prob_grad, axis=0, keepdims=True)
            return total, along

        zero = jnp.zeros((1, PAIR * rows), jnp.float32)
        total, along = over_blocks(middle, (zero, zero))
        inverse = 1.0 / total
        delta = along * inverse

        def last(b, carry):
            probs = s_buf[span(b), : PAIR * rows] * inverse
            score_grad = probs * (p_buf[span(b), :] - delta)
            p_low[span(b), columns_of(pair)] = probs.astype(jnp.bfloat16)
            d_low[span(b), columns_of(pair)] = score_grad.astype(jnp.bfloat16)
            return carry

        over_blocks(last, 0)
        return carry

    lax.fori_loop(0, pairs, backward_pair, 0)

    def rows_at(index):
        return pl.ds(pl.multiple_of(index * rows, rows), rows)

    def terms(index):
        key_part = dot(d_low[rows_at(index), :], q_stack[...])
        value_part = dot(p_low[rows_at(index), :], g_stack[...])
        return key_part, value_part

    def reduce_copy(step):
        return remote(
            part_out.at[step - 1],
            part_in.at[step - 1],
            red_send.at[step - 1],
            red_recv.at[step - 1],
            (s, lax.rem(f + n_f - step, n_f), t),
        )

    for step in range(n_f - 1, 0, -1):

        @pl.when(f - step >= 0)
        def _(step=step):
            key_part, value_part = terms(lax.rem(f + n_f - step, n_f))
            part_out[step - 1, 0] = key_part.astype(jnp.bfloat16)
            part_out[step - 1, 1] = value_part.astype(jnp.bfloat16)
            reduce_copy(step).start()

    turn(kv_held, 0, turned_held)

    def query_pair(pair, carry):
        def step(b, query_sum):
            return query_sum + dot(turned_held[:, span(b)], d_low[span(b), columns_of(pair)])

        query_sum = over_blocks(step, jnp.zeros((HEAD_DIM, PAIR * rows), jnp.float32))
        dq_ref[0, :, lanes_of(pair)] = untangled(query_sum * SCALE)
        return carry

    lax.fori_loop(0, pairs, query_pair, 0)
    lax.fori_loop(wides // 2, wides, forward_pair, 0)

    key_sum, value_sum = terms(f)
    sums[0] = key_sum
    sums[1] = value_sum
    for step in range(1, n_f):

        @pl.when(f + step < n_f)
        def _(step=step):
            reduce_copy(step).wait_recv()
            sums[...] += part_in[step - 1].astype(jnp.float32)

    dk_ref[0] = (sums[0] * SCALE).astype(jnp.bfloat16)
    dv_ref[0] = sums[1].astype(jnp.bfloat16)
    for copy in first:
        copy.wait_send()

    @pl.when(lane == 0)
    def _():
        for copy in fwd_copies(0, sibling):
            copy.wait_send()

    for step in range(1, n_high):

        @pl.when(high + step < n_high)
        def _(step=step):
            for copy in across(step):
                copy.wait_send()

        @pl.when(high - step >= 0)
        def _(step=step):
            passed_on(step).wait_send()

    for step in range(1, n_f):

        @pl.when(f + step < n_f)
        def _(step=step):
            for copy in fwd_ids(step) + held_copies(step):
                copy.wait_send()

        @pl.when(f - step >= 0)
        def _(step=step):
            reduce_copy(step).wait_send()

    for pair in range(pairs):
        for step in range(n_t):
            query_copy(pair, step).wait_send()


def hand_over(*refs):
    count = len(refs) // 2
    sems = refs[-1]
    copies = [
        pltpu.make_async_copy(refs[i], refs[count + i], sems.at[i]) for i in range(count)
    ]
    for copy in copies:
        copy.start()
    for copy in copies:
        copy.wait()


def local(sizes, *arrays):
    n_s, n_f, n_t = sizes
    queries, key_rows = arrays[0], arrays[1]
    rows, width = queries.shape[1], queries.shape[2]
    pairs = width // (PAIR * HEAD_DIM)
    seq = n_f * rows
    low, full = jnp.bfloat16, jnp.float32
    dma = pltpu.SemaphoreType.DMA
    anywhere = pl.BlockSpec(memory_space=pl.ANY)
    inside = pl.BlockSpec(memory_space=pltpu.VMEM)
    elements = rows * (width // HEAD_DIM) * seq
    results = pl.pallas_call(
        functools.partial(kernel, n_s, n_f, n_t),
        out_shape=[
            pltpu.VMEM(queries.shape, low),
            pltpu.VMEM(queries.shape, low),
            pltpu.VMEM(key_rows.shape, low),
            pltpu.VMEM(key_rows.shape, low),
        ],
        in_specs=[anywhere] * 9,
        out_specs=[inside] * 4,
        scratch_shapes=[
            pltpu.VMEM((rows, width), low),
            pltpu.VMEM((rows, width), low),
            pltpu.VMEM((n_f, 2, rows, HEAD_DIM), low),
            pltpu.VMEM((n_f, 1, rows), jnp.int32),
            pltpu.VMEM((pairs, rows, PAIR * HEAD_DIM), low),
            pltpu.VMEM((n_f, 2, rows, HEAD_DIM), low),
            pltpu.VMEM((n_f, 1, rows), jnp.int32),
            pltpu.VMEM((seq, rows), full),
            pltpu.VMEM((seq, rows), full),
            pltpu.VMEM((HEAD_DIM, seq), low),
            pltpu.VMEM((HEAD_DIM, seq), low),
            pltpu.VMEM((seq, WIDE * rows), full),
            pltpu.VMEM((seq, PAIR * rows), full),
            pltpu.VMEM((seq, pairs * PAIR * rows), low),
            pltpu.VMEM((seq, pairs * PAIR * rows), low),
            pltpu.VMEM((pairs * PAIR * rows, HEAD_DIM), low),
            pltpu.VMEM((pairs * PAIR * rows, HEAD_DIM), low),
            pltpu.VMEM((n_f - 1, 2, rows, HEAD_DIM), low),
            pltpu.VMEM((n_f - 1, 2, rows, HEAD_DIM), low),
            pltpu.VMEM((2, rows, HEAD_DIM), full),
            dma((5,)),
            dma((n_f // LOW, 2)),
            dma((n_f // LOW, 2)),
            dma((2 * n_t + 1,)),
            dma((2 * n_t + 1,)),
            dma((n_f - 1,)),
            dma((n_f - 1,)),
            dma((n_f // LOW - 1,)),
            dma((n_f // LOW - 1,)),
            dma((n_f - 1, 2)),
            dma((n_f - 1, 2)),
            dma((pairs, n_t)),
            dma((pairs, n_t)),
            dma((n_f - 1,)),
            dma((n_f - 1,)),
        ],
        compiler_params=pltpu.CompilerParams(
            collective_id=0, has_side_effects=True, vmem_limit_bytes=VMEM_BYTES
        ),
        cost_estimate=pl.CostEstimate(
            flops=14 * elements * HEAD_DIM,
            bytes_accessed=6 * rows * width * 2,
            transcendentals=2 * elements,
        ),
        name="tick",
    )(*arrays)
    return pl.pallas_call(
        hand_over,
        out_shape=[pltpu.HBM(result.shape, low) for result in results],
        in_specs=[inside] * len(results),
        out_specs=[anywhere] * len(results),
        scratch_shapes=[dma((len(results),))],
        compiler_params=pltpu.CompilerParams(vmem_limit_bytes=VMEM_BYTES // 4),
        name="hand_over",
    )(*results)


def solution(mesh):
    sizes = (mesh.shape["section"], mesh.shape["fsdp"], mesh.shape["tp"])
    by_head = P("section", "fsdp", "tp")
    by_row = P("section", ("fsdp", "tp"), None)
    ids = P("section", "fsdp")
    return jax.shard_map(
        functools.partial(local, sizes),
        mesh=mesh,
        in_specs=(by_head, by_head, by_head, ids, by_row, by_row, by_row, ids, by_head),
        out_specs=(by_head,) * 4,
        check_vma=False,
    )
```

```python
import functools
import math

import jax
import jax.numpy as jnp
from jax import lax
from jax.experimental import pallas as pl
from jax.experimental.pallas import tpu as pltpu
from jax.sharding import PartitionSpec as P

HEAD_DIM = 128
PAIR = 2
LOW = 2
WIDE = 4
NEG = -1e30
SCALE = 1.0 / math.sqrt(HEAD_DIM)
SCALE_LOG2 = SCALE * math.log2(math.e)
MESH = pl.DeviceIdType.MESH
VMEM_BYTES = 63 * 1024 * 1024

NT = (((1,), (1,)), ((), ()))


def dot(left, right, dims=(((1,), (0,)), ((), ()))):
    return lax.dot_general(left, right, dims, preferred_element_type=jnp.float32)


def kernel(
    n_s,
    n_f,
    n_t,
    q_ref,
    k_ref,
    v_ref,
    sg_ref,
    hq_ref,
    hk_ref,
    hv_ref,
    hs_ref,
    do_ref,
    o_ref,
    dq_ref,
    dk_ref,
    dv_ref,
    q_buf,
    g_buf,
    kv_fwd,
    sg_fwd,
    hq_buf,
    kv_held,
    sg_held,
    bias,
    bias_held,
    turned,
    turned_held,
    s_buf,
    p_buf,
    p_low,
    d_low,
    q_stack,
    g_stack,
    part_out,
    part_in,
    sums,
    local_sem,
    fwd_send,
    fwd_recv,
    one_send,
    one_recv,
    ids_send,
    ids_recv,
    on_send,
    on_recv,
    two_send,
    two_recv,
    hq_send,
    hq_recv,
    red_send,
    red_recv,
):
    rows = q_ref.shape[1]
    part_rows = hq_ref.shape[1]
    width = q_ref.shape[2]
    pair_width = PAIR * HEAD_DIM
    pairs = width // pair_width
    seq = n_f * rows
    block = min(512, seq)
    blocks = seq // block

    s, f, t = lax.axis_index("section"), lax.axis_index("fsdp"), lax.axis_index("tp")
    mirror = n_s - 1 - s

    def at_f(step):
        return lax.rem(f + step, n_f)

    high = f // LOW
    lane = f - high * LOW
    n_high = n_f // LOW
    sibling = high * LOW + (LOW - 1 - lane)

    def at_t(step):
        return lax.rem(t + step, n_t)

    for b in range(n_f):

        @pl.when(f < b)
        def _(b=b):
            for kv, ids in ((kv_fwd, sg_fwd), (kv_held, sg_held)):
                kv[b] = jnp.zeros_like(kv[b])
                ids[b] = jnp.zeros_like(ids[b])

    local = [
        pltpu.make_async_copy(k_ref.at[0], kv_fwd.at[f, 0], local_sem.at[0]),
        pltpu.make_async_copy(v_ref.at[0], kv_fwd.at[f, 1], local_sem.at[1]),
        pltpu.make_async_copy(sg_ref, sg_fwd.at[f], local_sem.at[2]),
        pltpu.make_async_copy(q_ref.at[0], q_buf, local_sem.at[3]),
        pltpu.make_async_copy(do_ref.at[0], g_buf, local_sem.at[4]),
    ]
    for copy in local:
        copy.start()

    barrier = pltpu.get_barrier_semaphore()
    for step in range(n_t):
        pl.semaphore_signal(
            barrier, inc=1, device_id=(mirror, f, at_t(step)), device_id_type=MESH
        )
    for step in range(1, n_f):
        pl.semaphore_signal(barrier, inc=1, device_id=(s, at_f(step), t), device_id_type=MESH)
    pl.semaphore_wait(barrier, n_t + n_f - 1)

    def remote(src, dst, send_sem, recv_sem, device):
        return pltpu.make_async_remote_copy(
            src_ref=src,
            dst_ref=dst,
            send_sem=send_sem,
            recv_sem=recv_sem,
            device_id=device,
            device_id_type=MESH,
        )

    own_rows = pl.ds(pl.multiple_of(t * part_rows, part_rows), part_rows)

    first = []
    for step in range(n_t):
        to = at_t(step)
        columns = pl.ds(pl.multiple_of(to * HEAD_DIM, HEAD_DIM), HEAD_DIM)
        for which, held in enumerate((hk_ref, hv_ref)):
            first.append(
                remote(
                    held.at[0, :, columns],
                    kv_held.at[f, which, own_rows, :],
                    one_send.at[2 * step + which],
                    one_recv.at[2 * step + which],
                    (mirror, f, to),
                )
            )
    first.append(
        remote(
            hs_ref,
            sg_held.at[f],
            one_send.at[2 * n_t],
            one_recv.at[2 * n_t],
            (mirror, f, t),
        )
    )
    for copy in first:
        copy.start()

    def query_copy(pair, step):
        to = at_t(step)
        columns = pl.ds(
            pl.multiple_of(to * width + pair * pair_width, pair_width), pair_width
        )
        return remote(
            hq_ref.at[0, :, columns],
            hq_buf.at[pair, own_rows, :],
            hq_send.at[pair, step],
            hq_recv.at[pair, step],
            (mirror, f, to),
        )

    def send_queries(begin, end):
        for pair in range(begin, end):
            for step in range(n_t):
                query_copy(pair, step).start()

    send_queries(0, 1)

    def fwd_copies(at, device):
        return [
            remote(
                src.at[0],
                kv_fwd.at[f, which],
                fwd_send.at[at, which],
                fwd_recv.at[at, which],
                (s, device, t),
            )
            for which, src in enumerate((k_ref, v_ref))
        ]

    def across(step):
        return fwd_copies(step, lax.rem(high + step, n_high) * LOW + lane)

    def passed_on(step):
        block_at = lax.rem(high + n_high - step, n_high) * LOW + lane
        return remote(
            kv_fwd.at[block_at],
            kv_fwd.at[block_at],
            on_send.at[step - 1],
            on_recv.at[step - 1],
            (s, sibling, t),
        )

    def fwd_ids(step):
        return [
            remote(
                sg_ref,
                sg_fwd.at[f],
                ids_send.at[step - 1],
                ids_recv.at[step - 1],
                (s, at_f(step), t),
            )
        ]

    def send_later(copies_of):
        for step in range(n_f - 1, 0, -1):

            @pl.when(f + step < n_f)
            def _(step=step):
                for copy in copies_of(step):
                    copy.start()

    def take_earlier(copies_of):
        for step in range(1, n_f):

            @pl.when(f - step >= 0)
            def _(step=step):
                for copy in copies_of(step):
                    copy.wait_recv()

    for step in range(n_high - 1, 0, -1):

        @pl.when(high + step < n_high)
        def _(step=step):
            for copy in across(step):
                copy.start()


    for copy in first:
        copy.wait_recv()
    def held_copies(step):
        return [
            remote(
                buffer.at[f],
                buffer.at[f],
                two_send.at[step - 1, which],
                two_recv.at[step - 1, which],
                (s, at_f(step), t),
            )
            for which, buffer in enumerate((kv_held, sg_held))
        ]

    send_later(held_copies)

    @pl.when(lane == 0)
    def _():
        for copy in fwd_copies(0, sibling):
            copy.start()

    send_later(fwd_ids)

    send_queries(1, 2)

    for step in range(1, n_high):

        @pl.when(high - step >= 0)
        def _(step=step):
            for copy in across(step):
                copy.wait_recv()
            passed_on(step).start()

    send_queries(2, pairs)


    def make_bias(ids, bias):
        own = ids[f]
        for b in range(n_f):
            key_ids = jnp.transpose(jnp.broadcast_to(ids[b], (rows, rows)))
            key_pos = b * rows + lax.broadcasted_iota(jnp.int32, (rows, rows), 0)
            own_pos = f * rows + lax.broadcasted_iota(jnp.int32, (rows, rows), 1)
            seen = (key_pos <= own_pos) & (key_ids == own)
            bias[b * rows : (b + 1) * rows, :] = jnp.where(seen, 0.0, NEG)

    def over_blocks(step, start):
        if blocks == 1:
            return step(0, start)
        return lax.fori_loop(0, blocks, step, start)

    def span(b):
        if blocks == 1:
            return pl.ds(0, block)
        return pl.ds(pl.multiple_of(b * block, block), block)

    def piece(kv, which, b):
        per = block // rows
        if blocks == 1:
            part = kv[:, which]
        else:
            part = kv[pl.ds(b * per, per), which]
        return part.reshape(block, HEAD_DIM)

    def turn(kv, which, turned):
        for b in range(n_f):
            turned[:, b * rows : (b + 1) * rows] = jnp.transpose(kv[b, which])

    def stacked(pair_block):
        return jnp.concatenate(
            [
                pair_block[:, h * HEAD_DIM : (h + 1) * HEAD_DIM]
                for h in range(pair_block.shape[1] // HEAD_DIM)
            ],
            axis=0,
        )

    def scores_of(kv, query, bias, at=0):
        def step(b, top):
            masked = jnp.concatenate([bias[span(b), :]] * (query.shape[0] // rows), axis=1)
            scores = dot(piece(kv, 0, b), query, NT) * SCALE_LOG2 + masked
            s_buf[span(b), at : at + query.shape[0]] = scores
            return jnp.maximum(top, jnp.max(scores, axis=0, keepdims=True))

        return over_blocks(step, jnp.full((1, query.shape[0]), NEG, jnp.float32))

    def untangled(wide):
        return jnp.concatenate(
            [
                jnp.transpose(wide[:, h * rows : (h + 1) * rows])
                for h in range(wide.shape[1] // rows)
            ],
            axis=1,
        ).astype(jnp.bfloat16)

    def lanes_of(pair):
        if isinstance(pair, int):
            return pl.ds(pair * pair_width, pair_width)
        return pl.ds(pl.multiple_of(pair * pair_width, pair_width), pair_width)

    for copy in local:
        copy.wait()
    take_earlier(fwd_ids)
    make_bias(sg_fwd, bias)

    @pl.when(lane == LOW - 1)
    def _():
        for copy in fwd_copies(0, sibling):
            copy.wait_recv()

    for step in range(1, n_high):

        @pl.when(high - step >= 0)
        def _(step=step):
            passed_on(step).wait_recv()

    turn(kv_fwd, 1, turned)

    def wide_lanes(index):
        return pl.ds(pl.multiple_of(index * WIDE * HEAD_DIM, WIDE * HEAD_DIM), WIDE * HEAD_DIM)

    def forward_pair(index, carry):
        query = stacked(q_buf[:, wide_lanes(index)])
        top = scores_of(kv_fwd, query, bias)

        def step(b, sums):
            total, out = sums
            weights = jnp.exp2(s_buf[span(b), : WIDE * rows] - top)
            total = total + jnp.sum(weights, axis=0, keepdims=True)
            out = out + dot(turned[:, span(b)], weights.astype(jnp.bfloat16))
            return total, out

        total, out = over_blocks(
            step,
            (
                jnp.zeros((1, WIDE * rows), jnp.float32),
                jnp.zeros((HEAD_DIM, WIDE * rows), jnp.float32),
            ),
        )
        o_ref[0, :, wide_lanes(index)] = untangled(out * (1.0 / total))
        return carry

    wides = width // (WIDE * HEAD_DIM)
    lax.fori_loop(0, wides // 2, forward_pair, 0)

    take_earlier(held_copies)
    make_bias(sg_held, bias_held)

    def columns_of(pair):
        if isinstance(pair, int):
            return pl.ds(pair * PAIR * rows, PAIR * rows)
        return pl.ds(pl.multiple_of(pair * (PAIR * rows), PAIR * rows), PAIR * rows)

    def backward_pair(pair, carry):
        half = pair % (WIDE // PAIR) * (PAIR * rows)
        grad = stacked(g_buf[:, lanes_of(pair)])
        g_stack[columns_of(pair), :] = grad
        for step in range(n_t):
            query_copy(pair, step).wait_recv()
        query = stacked(hq_buf[pair])
        q_stack[columns_of(pair), :] = query
        top = scores_of(kv_held, query, bias_held, half)

        def middle(b, sums):
            total, along = sums
            weights = jnp.exp2(s_buf[span(b), half : half + PAIR * rows] - top)
            prob_grad = dot(piece(kv_held, 1, b), grad, NT)
            s_buf[span(b), half : half + PAIR * rows] = weights
            p_buf[span(b), half : half + PAIR * rows] = prob_grad
            total = total + jnp.sum(weights, axis=0, keepdims=True)
            along = along + jnp.sum(weights * prob_grad, axis=0, keepdims=True)
            return total, along

        zero = jnp.zeros((1, PAIR * rows), jnp.float32)
        total, along = over_blocks(middle, (zero, zero))
        inverse = 1.0 / total
        delta = along * inverse

        def last(b, carry):
            probs = s_buf[span(b), half : half + PAIR * rows] * inverse
            score_grad = probs * (p_buf[span(b), half : half + PAIR * rows] - delta)
            p_low[span(b), columns_of(pair)] = probs.astype(jnp.bfloat16)
            d_low[span(b), columns_of(pair)] = score_grad.astype(jnp.bfloat16)
            return carry

        over_blocks(last, 0)
        return carry

    for pair in range(pairs):
        backward_pair(pair, 0)

    def rows_at(index):
        return pl.ds(pl.multiple_of(index * rows, rows), rows)

    def terms(index):
        key_part = dot(d_low[rows_at(index), :], q_stack[...])
        value_part = dot(p_low[rows_at(index), :], g_stack[...])
        return key_part, value_part

    def reduce_copy(step):
        return remote(
            part_out.at[step - 1],
            part_in.at[step - 1],
            red_send.at[step - 1],
            red_recv.at[step - 1],
            (s, lax.rem(f + n_f - step, n_f), t),
        )

    for step in range(n_f - 1, 0, -1):

        @pl.when(f - step >= 0)
        def _(step=step):
            key_part, value_part = terms(lax.rem(f + n_f - step, n_f))
            part_out[step - 1, 0] = key_part.astype(jnp.bfloat16)
            part_out[step - 1, 1] = value_part.astype(jnp.bfloat16)
            reduce_copy(step).start()

    turn(kv_held, 0, turned_held)

    def query_pair(pair, carry):
        def step(b, query_sum):
            return query_sum + dot(turned_held[:, span(b)], d_low[span(b), columns_of(pair)])

        query_sum = over_blocks(step, jnp.zeros((HEAD_DIM, PAIR * rows), jnp.float32))
        dq_ref[0, :, lanes_of(pair)] = untangled(query_sum * SCALE)
        return carry

    lax.fori_loop(0, pairs, query_pair, 0)
    lax.fori_loop(wides // 2, wides, forward_pair, 0)

    key_sum, value_sum = terms(f)
    sums[0] = key_sum
    sums[1] = value_sum
    for step in range(1, n_f):

        @pl.when(f + step < n_f)
        def _(step=step):
            reduce_copy(step).wait_recv()
            sums[...] += part_in[step - 1].astype(jnp.float32)

    dk_ref[0] = (sums[0] * SCALE).astype(jnp.bfloat16)
    dv_ref[0] = sums[1].astype(jnp.bfloat16)
    for copy in first:
        copy.wait_send()

    @pl.when(lane == 0)
    def _():
        for copy in fwd_copies(0, sibling):
            copy.wait_send()

    for step in range(1, n_high):

        @pl.when(high + step < n_high)
        def _(step=step):
            for copy in across(step):
                copy.wait_send()

        @pl.when(high - step >= 0)
        def _(step=step):
            passed_on(step).wait_send()

    for step in range(1, n_f):

        @pl.when(f + step < n_f)
        def _(step=step):
            for copy in fwd_ids(step) + held_copies(step):
                copy.wait_send()

        @pl.when(f - step >= 0)
        def _(step=step):
            reduce_copy(step).wait_send()

    for pair in range(pairs):
        for step in range(n_t):
            query_copy(pair, step).wait_send()


def hand_over(*refs):
    count = len(refs) // 2
    sems = refs[-1]
    copies = [
        pltpu.make_async_copy(refs[i], refs[count + i], sems.at[i]) for i in range(count)
    ]
    for copy in copies:
        copy.start()
    for copy in copies:
        copy.wait()


def local(sizes, *arrays):
    n_s, n_f, n_t = sizes
    queries, key_rows = arrays[0], arrays[1]
    rows, width = queries.shape[1], queries.shape[2]
    pairs = width // (PAIR * HEAD_DIM)
    seq = n_f * rows
    low, full = jnp.bfloat16, jnp.float32
    dma = pltpu.SemaphoreType.DMA
    anywhere = pl.BlockSpec(memory_space=pl.ANY)
    inside = pl.BlockSpec(memory_space=pltpu.VMEM)
    elements = rows * (width // HEAD_DIM) * seq
    results = pl.pallas_call(
        functools.partial(kernel, n_s, n_f, n_t),
        out_shape=[
            pltpu.VMEM(queries.shape, low),
            pltpu.VMEM(queries.shape, low),
            pltpu.VMEM(key_rows.shape, low),
            pltpu.VMEM(key_rows.shape, low),
        ],
        in_specs=[anywhere] * 9,
        out_specs=[inside] * 4,
        scratch_shapes=[
            pltpu.VMEM((rows, width), low),
            pltpu.VMEM((rows, width), low),
            pltpu.VMEM((n_f, 2, rows, HEAD_DIM), low),
            pltpu.VMEM((n_f, 1, rows), jnp.int32),
            pltpu.VMEM((pairs, rows, PAIR * HEAD_DIM), low),
            pltpu.VMEM((n_f, 2, rows, HEAD_DIM), low),
            pltpu.VMEM((n_f, 1, rows), jnp.int32),
            pltpu.VMEM((seq, rows), full),
            pltpu.VMEM((seq, rows), full),
            pltpu.VMEM((HEAD_DIM, seq), low),
            pltpu.VMEM((HEAD_DIM, seq), low),
            pltpu.VMEM((seq, WIDE * rows), full),
            pltpu.VMEM((seq, WIDE * rows), full),
            pltpu.VMEM((seq, pairs * PAIR * rows), low),
            pltpu.VMEM((seq, pairs * PAIR * rows), low),
            pltpu.VMEM((pairs * PAIR * rows, HEAD_DIM), low),
            pltpu.VMEM((pairs * PAIR * rows, HEAD_DIM), low),
            pltpu.VMEM((n_f - 1, 2, rows, HEAD_DIM), low),
            pltpu.VMEM((n_f - 1, 2, rows, HEAD_DIM), low),
            pltpu.VMEM((2, rows, HEAD_DIM), full),
            dma((5,)),
            dma((n_f // LOW, 2)),
            dma((n_f // LOW, 2)),
            dma((2 * n_t + 1,)),
            dma((2 * n_t + 1,)),
            dma((n_f - 1,)),
            dma((n_f - 1,)),
            dma((n_f // LOW - 1,)),
            dma((n_f // LOW - 1,)),
            dma((n_f - 1, 2)),
            dma((n_f - 1, 2)),
            dma((pairs, n_t)),
            dma((pairs, n_t)),
            dma((n_f - 1,)),
            dma((n_f - 1,)),
        ],
        compiler_params=pltpu.CompilerParams(
            collective_id=0, has_side_effects=True, vmem_limit_bytes=VMEM_BYTES
        ),
        cost_estimate=pl.CostEstimate(
            flops=14 * elements * HEAD_DIM,
            bytes_accessed=6 * rows * width * 2,
            transcendentals=2 * elements,
        ),
        name="tick",
    )(*arrays)
    return pl.pallas_call(
        hand_over,
        out_shape=[pltpu.HBM(result.shape, low) for result in results],
        in_specs=[inside] * len(results),
        out_specs=[anywhere] * len(results),
        scratch_shapes=[dma((len(results),))],
        compiler_params=pltpu.CompilerParams(vmem_limit_bytes=VMEM_BYTES // 4),
        name="hand_over",
    )(*results)


def solution(mesh):
    sizes = (mesh.shape["section"], mesh.shape["fsdp"], mesh.shape["tp"])
    by_head = P("section", "fsdp", "tp")
    by_row = P("section", ("fsdp", "tp"), None)
    ids = P("section", "fsdp")
    return jax.shard_map(
        functools.partial(local, sizes),
        mesh=mesh,
        in_specs=(by_head, by_head, by_head, ids, by_row, by_row, by_row, ids, by_head),
        out_specs=(by_head,) * 4,
        check_vma=False,
    )
```
